512 devices in a mesh: seq: 16 (over z, x_hi), dp: 32 (over y, x_lo, core).
Axes of the slice: x: 4 (x_hi: 2, x_lo: 2; x = x_hi * 2 + x_lo), y: 8, z: 8, core: 2. Of those that a mesh axis runs over, the one named last changes fastest.
Arguments:
- inputs: bfloat16 [32, 2048, 4096], P('dp', 'seq'), may hold values from -6 to 6
- weights: bfloat16 [4096, 768], P(('seq', 'dp')), may hold values from -0.09375 to 0.09375
- lengths: int32 [32, 8], P('dp'), may hold values from 1 to 1024, 2048 in all within a row
- cotangent: bfloat16 [32, 2048, 256], P('dp', 'seq'), may hold values from -6 to 6
Outputs:
- normed: bfloat16 [32, 2048, 256], P('dp', 'seq')
- grad_inputs: bfloat16 [32, 2048, 4096], P('dp', 'seq')
- grad_weights: bfloat16 [4096, 768], P(('seq', 'dp'))
The draws below stay inside these ranges and needn't reach their ends.
Inputs may be any that keep to these rules, and one draw needn't show every extreme that they name: Row b holds the lengths of the 8 documents packed end to end into sequence b; they sum to 2048.
All inputs are finite; a program needn't handle non-finite values.
Results may differ from the reference program's by a relative error of at most 0.03.
Values may be sent and summed in bfloat16 or wider, within the bound.
A program may use at most 64 MiB of HBM per device.

```python
import math
import jax
import jax.numpy as jnp
import numpy as np
from jax import lax

D = 4096
HEAD = 128
HEADS = 2
NDOC = 8
SEQ = 2048
SEQS = 32


def spiked(drawn, stream_key, source, target, shards_of, factor):
    def block_of(axis_at):
        return (jnp.arange(drawn.shape[axis_at]) // (drawn.shape[axis_at] // shards_of)).reshape((-1,) + (1,) * (drawn.ndim - 1 - axis_at))

    one_side = jax.random.permutation(stream_key, shards_of)[block_of(target)]
    second = (block_of(target) + shards_of // 2) % shards_of
    return jnp.where((block_of(source) == one_side) | (block_of(source) == second), factor * drawn, drawn)


def level_of(rng, extent, split, least, high):
    factor_of = 1.0
    for dim, shards_of in split:
        steps = jax.random.uniform(jax.random.fold_in(jax.random.fold_in(rng, 6), dim), (shards_of,), jnp.float32, least / len(split), high / len(split))
        factor_of = factor_of * jnp.repeat(jnp.exp(steps), extent[dim] // shards_of).reshape((-1,) + (1,) * (len(extent) - 1 - dim))
    return factor_of


def length_profile(number_of, total, most, skew):
    portions = [(1 << 20) // math.isqrt(grade ** skew) + 1 for grade in range(2, number_of + 1)]
    rest, given = total - most - (number_of - 1), [1] * (number_of - 1)
    while rest > 0:
        candidates = [i for i in range(number_of - 1) if given[i] < most]
        mass, budget = sum([portions[i] for i in candidates]), rest
        for i in candidates:
            more = min(most - given[i], max(1, budget * portions[i] // mass), rest)
            given[i] = given[i] + more
            rest = rest - more
    return np.array([most] + given)


def uneven(stream_key, count, total, reach, skew):
    if count == 2:
        one = jax.random.randint(stream_key, (), max(1, total - reach), min(reach, total - 1) + 1)
        return jnp.stack([one, total - one])
    sizes = jnp.asarray(length_profile(count, total, reach, skew), jnp.int32)
    pairs = (count - 1) // 2
    donor, receiver = sizes[1:1 + 2 * pairs:2], sizes[2:2 + 2 * pairs:2]
    margin = jnp.minimum(donor - 1, reach - receiver)
    passed = jax.random.randint(jax.random.fold_in(stream_key, 1), (pairs,), 0, 1 << 20) % (margin + 1)
    sizes = sizes.at[1:1 + 2 * pairs:2].set(donor - passed).at[2:2 + 2 * pairs:2].set(receiver + passed)
    return sizes[jax.random.permutation(jax.random.fold_in(stream_key, 2), count)]


def centred(own_key, shape, width, limit, cuts=(), kind=jnp.bfloat16):
    loudness = level_of(own_key, shape, cuts, -0.22, 0.18) if cuts else 1.0
    values = jax.random.normal(own_key, shape, jnp.float32) * width * loudness
    return jnp.minimum(jnp.maximum(values, -limit), limit).astype(kind)


def noise_with(key, dims, scale, limit, shards, heavy, held_as=jnp.bfloat16):
    entries = scale * jax.random.normal(key, dims, jnp.float32)
    if shards:
        entries = entries * level_of(key, dims, shards, -0.22, 0.18)
    return jnp.clip(spiked(entries, jax.random.fold_in(key, 3), *heavy), -limit, limit).astype(held_as)


def setup_inputs(seed: int = 0) -> dict:
    streams_of = jax.random.split(jax.random.key(seed), 5)
    inputs = noise_with(streams_of[0], (SEQS, SEQ, D), 1.0, 6.0, ((0, 32), (1, 16)), (1, 2, 16, 2.0))
    weights = centred(streams_of[1], (D, 3 * HEADS * HEAD), D ** -0.5, 0.09375, ((0, 512),))
    lengths = jax.vmap(lambda own: uneven(own, NDOC, SEQ, SEQ // 2, 2))(jax.random.split(streams_of[2], SEQS)).reshape((SEQS, NDOC)).astype(jnp.int32)
    cotangent = centred(streams_of[3], (SEQS, SEQ, HEADS * HEAD), 1.0, 6.0, ((0, 32), (1, 16)))
    return {"inputs": inputs, "weights": weights, "lengths": lengths, "cotangent": cotangent}


epsilon = 1.0
highest = lax.Precision.HIGHEST

def document(lengths_row, positions):
    ends = jnp.cumsum(lengths_row)
    starts = ends - lengths_row
    return lax.optimization_barrier(jnp.sum((starts[None, :] <= positions[:, None]).astype(jnp.int32), axis=1)) - 1

def make_sequence(weights):

    def one_sequence(packed):
        tokens, lengths_row, upstream_raw = packed
        span = HEADS * HEAD
        shrink = 1.0 / HEAD
        positions = jnp.arange(SEQ, dtype=jnp.int32)
        docs = document(lengths_row, positions)
        linked = (docs[:, None] == docs[None, :]) & (positions[None, :] <= positions[:, None])
        projected = jnp.dot(tokens, weights, preferred_element_type=jnp.float32).astype(jnp.bfloat16)
        query = projected[:, :span].reshape(SEQ, HEADS, HEAD).astype(jnp.float32)
        keys = projected[:, span:2 * span].reshape(SEQ, HEADS, HEAD).astype(jnp.float32)
        values = projected[:, 2 * span:].reshape(SEQ, HEADS, HEAD).astype(jnp.float32)
        scores = jnp.where(linked[None], shrink * jnp.einsum('thd,jhd->htj', query, keys, precision=highest), 0.0)
        attended = jnp.einsum('htj,jhd->thd', scores, values, precision=highest)
        inverse = lax.rsqrt(lax.optimization_barrier(jnp.mean(attended * attended, axis=2, keepdims=True)) + epsilon)
        normed = (attended * inverse).astype(jnp.bfloat16).reshape(SEQ, span)
        upstream = upstream_raw.reshape(SEQ, HEADS, HEAD).astype(jnp.float32)
        along = lax.optimization_barrier(jnp.mean(upstream * attended, axis=2, keepdims=True))
        grad_attended = (inverse * upstream - attended * inverse * inverse * inverse * along).astype(jnp.bfloat16)
        grad_wide = grad_attended.astype(jnp.float32)
        mixed = jnp.where(linked[None], shrink * jnp.einsum('the,jhe->htj', grad_wide, values, precision=highest), 0.0)
        grad_query = jnp.einsum('htj,jhd->thd', mixed, keys, precision=highest)
        grad_keys = jnp.einsum('htj,thd->jhd', mixed, query, precision=highest)
        grad_values = jnp.einsum('htj,the->jhe', scores, grad_wide, precision=highest)
        grad_all = jnp.concatenate([grad_query.reshape(SEQ, span), grad_keys.reshape(SEQ, span), grad_values.reshape(SEQ, span)], axis=1).astype(jnp.bfloat16)
        grad_inputs = jnp.dot(grad_all, weights.T, preferred_element_type=jnp.float32).astype(jnp.bfloat16)
        factor = 1.0 / math.sqrt(SEQS * SEQ)
        summed = jnp.dot(tokens.astype(jnp.float32).T, grad_all.astype(jnp.float32), precision=highest)
        replica = (factor * summed).astype(jnp.bfloat16)
        return (normed, grad_inputs, replica)
    return one_sequence

def reference(inputs, weights, lengths, cotangent):
    normed, grad_inputs, replicas = lax.map(make_sequence(weights), (inputs, lengths, cotangent))
    grad_weights = lax.optimization_barrier(jnp.sum(replicas.astype(jnp.float32), axis=0)).astype(jnp.bfloat16)
    return (normed, grad_inputs, grad_weights)
```

```python
import functools
import math

import jax
import jax.numpy as jnp
from jax import lax
from jax.experimental import pallas as pl
from jax.experimental.pallas import tpu as pltpu
from jax.sharding import PartitionSpec as P

HEAD = 128
NDOC = 8
ROWS = 16
MESH = pl.DeviceIdType.MESH
F32, BF16 = jnp.float32, jnp.bfloat16
ORDERS = (("x", "y", "z"), ("z", "x", "y"), ("y", "z", "x"))


def dot(a, b):
    return jnp.dot(a, b, preferred_element_type=F32)


def dot_nt(a, b):
    return lax.dot_general(a, b, (((1,), (1,)), ((), ())), preferred_element_type=F32)


def dot_tn(a, b):
    return lax.dot_general(a, b, (((0,), (0,)), ((), ())), preferred_element_type=F32)


def kernel(size, subs, tok, w, lens, cot, normed, gin, gw, *rest):
    (xsib, xt, wfull, wsend, wrecv, starts, csend, cots, proj, scan, keep, gbuf, mask, weak, hold, held, kept_n, nsend, nrecv,
     gown, gsend, grecv, dsend, drecv, send_sem, recv_sem) = rest[:26]
    wg, pg, ring, far, near = (rest[26 + 3 * i : 29 + 3 * i] for i in range(5))
    seqs = 2 * size["z"]
    rows = tok.shape[0]
    chunk = size["y"] * 2 * ROWS
    s, d = lax.axis_index("seq"), lax.axis_index("dp")
    c = lax.rem(d, 2)
    me = {"x": lax.rem(s, 2) * 2 + lax.rem(d // 2, 2), "y": d // 4, "z": s // 2}
    sibling = (s, d + 1 - 2 * c)

    def at(axis, place):
        spot = dict(me)
        spot[axis] = place
        return (spot["z"] * 2 + spot["x"] // 2, spot["y"] * 4 + lax.rem(spot["x"], 2) * 2 + c)

    def along(axis, step):
        return lax.rem(me[axis] + step + size[axis], size[axis])

    def remote(src, dst, index, target):
        return pltpu.make_async_remote_copy(
            src_ref=src,
            dst_ref=dst,
            send_sem=send_sem.at[index],
            recv_sem=recv_sem.at[index],
            device_id=target,
            device_id_type=MESH,
        )

    def drain(ref, sem):
        pltpu.make_async_copy(ref, ref, sem).wait()

    names = {}

    def number(*key):
        return names.setdefault(key, len(names))

    barrier = pltpu.get_barrier_semaphore()

    def greet(target):
        pl.semaphore_signal(barrier, inc=1, device_id=target, device_id_type=MESH)

    greet(sibling)
    for k in range(1, seqs):
        greet((lax.rem(s + k, seqs), d))
    for k in range(1, size["y"]):
        greet(at("y", along("y", k)))
    greet(at("x", along("x", 1)))
    greet(at("x", along("x", -1)))
    pl.semaphore_wait(barrier, 1 + seqs - 1 + size["y"] - 1 + 2)

    first = c == 0

    def head_columns(ref, part, mine):
        left = ref[:, part * 2 * HEAD : (2 * part + 1) * HEAD].astype(F32)
        right = ref[:, (2 * part + 1) * HEAD : (2 * part + 2) * HEAD].astype(F32)
        return jnp.where(first == mine, left, right)

    for p in range(3):
        wsend[:, p * HEAD : (p + 1) * HEAD] = head_columns(w, p, False)
    swap_w = remote(wsend, wrecv, number("w"), sibling)
    swap_w.start()
    swap_x = remote(tok, xsib, number("x"), sibling)
    swap_x.start()
    csend[...] = head_columns(cot, 0, False).astype(BF16)
    swap_c = remote(csend, cots.at[1], number("c"), sibling)
    swap_c.start()
    cots[0] = head_columns(cot, 0, True).astype(BF16)
    total = jnp.int32(0)
    for i in range(NDOC):
        starts[0, i] = jnp.full((8, HEAD), total.astype(F32))
        total = total + lens[0, i]
    swap_s = remote(starts.at[0], starts.at[1], number("s"), sibling)
    swap_s.start()

    swap_w.wait_recv()
    for p, (a1, a2, a3) in enumerate(ORDERS):
        mine = head_columns(w, p, True)
        other = wrecv[:, p * HEAD : (p + 1) * HEAD]
        both = jnp.where(first, jnp.concatenate([mine, other], 0), jnp.concatenate([other, mine], 0))
        wg[p][me[a3], me[a2], me[a1]] = both.astype(BF16)
        block = wg[p].at[me[a3], me[a2], me[a1]]
        index = number("g1", p)

        def one(k, _, block=block, a1=a1, index=index):
            remote(block, block, index, at(a1, along(a1, k))).start()
            return 0

        lax.fori_loop(1, size[a1], one, 0)

    def turn_own(i, _):
        at_chunk = pl.ds(pl.multiple_of(i * chunk, chunk), chunk)
        xt[at_chunk, 0:rows] = tok[:, at_chunk].T
        return 0

    def turn_sibling(i, _):
        at_chunk = pl.ds(pl.multiple_of(i * chunk, chunk), chunk)
        xt[at_chunk, rows : 2 * rows] = xsib[:, at_chunk].T
        return 0

    lax.fori_loop(0, seqs, turn_own, 0)
    for p, (a1, a2, a3) in enumerate(ORDERS):
        drain(wg[p].at[0, 0, pl.ds(0, size[a1] - 1)], recv_sem.at[number("g1", p)])
        block = wg[p].at[me[a3], me[a2]]
        index = number("g2", p)

        def two(k, _, block=block, a2=a2, index=index):
            remote(block, block, index, at(a2, along(a2, k))).start()
            return 0

        lax.fori_loop(1, size[a2], two, 0)
    swap_x.wait_recv()
    lax.fori_loop(0, seqs, turn_sibling, 0)

    def piece(p, sub):
        span = size[ORDERS[p][1]] // subs[p]
        return pl.ds(sub * span, span)

    def half(p, sign):
        return range(subs[p] // 2) if sign > 0 else range(subs[p] // 2, subs[p])

    lists = []
    for p in range(3):
        steps = size[ORDERS[p][2]] // 2
        for sign in (1, -1):
            hops = [(k, sub) for k in range(steps - 1) for sub in range(subs[p])]
            hops += [(steps - 1, sub) for sub in half(p, sign)]
            lists.append((p, sign, hops))
    going = {}
    waited = set()
    started = set()
    for turn in range(max(len(hops) for _, _, hops in lists)):
        for p, sign, hops in lists:
            if turn >= len(hops):
                continue
            k, sub = hops[turn]
            a1, a2, a3 = ORDERS[p]
            if p not in started:
                started.add(p)
                drain(wg[p].at[0, pl.ds(0, size[a2] - 1)], recv_sem.at[number("g2", p)])
            if k > 0:
                going[p, sign, k - 1, sub].wait_recv()
                waited.add((p, sign, k - 1, sub))
            block = wg[p].at[along(a3, -sign * k), piece(p, sub)]
            copy = remote(block, block, number("g3", p, sign, k, sub), at(a3, along(a3, sign)))
            copy.start()
            going[p, sign, k, sub] = copy

    swap_s.wait_recv()
    base = (s * rows).astype(F32)

    def count(b, positions):
        found = jnp.full(positions.shape, -1.0, F32)
        for i in range(NDOC):
            found = found + jnp.where(starts[b, i][None] <= positions, 1.0, 0.0)
        return found

    here = jnp.where(s < seqs // 2, starts[0], starts[1])

    def fill(r, _):
        low = (r * rows).astype(F32)
        inside = jnp.where((here >= low) & (here < low + rows), 1.0, 0.0)
        none = 1.0 - jnp.max(inside, axis=0)
        keep[r] = jnp.concatenate([none] * (keep.shape[1] // 8), axis=0)
        return 0

    lax.fori_loop(0, seqs, fill, 0)
    square = (rows // 8, 8, rows)
    by_row = lax.broadcasted_iota(jnp.int32, square, 0) * 8 + lax.broadcasted_iota(jnp.int32, square, 1)
    by_lane = lax.broadcasted_iota(jnp.int32, square, 2)

    def masks(b):
        docs_row = count(b, base + by_row.astype(F32))
        docs_lane = count(b, base + by_lane.astype(F32))
        linked = (docs_row == docs_lane) & (by_lane <= by_row)
        before = count(b, jnp.full((1, 8, HEAD), base - 1.0, F32))
        last = count(b, jnp.full((1, 8, HEAD), base + (rows - 1.0), F32))
        for i, found in enumerate((linked, docs_row == before, docs_row == last)):
            mask[b, i] = jnp.where(found, 1.0, 0.0).reshape(rows, rows)

    masks(0)
    masks(1)
    swap_c.wait_recv()
    for key, copy in going.items():
        if key not in waited:
            copy.wait_recv()
    for copy in going.values():
        copy.wait_send()
    for p, (a1, a2, a3) in enumerate(ORDERS):
        drain(wg[p].at[0, 0, pl.ds(0, size[a1] - 1)], send_sem.at[number("g1", p)])
        drain(wg[p].at[0, pl.ds(0, size[a2] - 1)], send_sem.at[number("g2", p)])
    for copy in (swap_w, swap_x, swap_c, swap_s):
        copy.wait_send()

    proj32 = gown

    def project(zz, acc):
        for xh in range(2):
            x2 = pl.ds(2 * xh, 2)
            parts = [
                wg[0][zz, :, x2].reshape(chunk, HEAD),
                wg[1][:, x2, zz].reshape(chunk, HEAD),
                jnp.stack([wg[2][2 * xh, zz], wg[2][2 * xh + 1, zz]], axis=1).reshape(chunk, HEAD),
            ]
            piece_w = jnp.concatenate(parts, axis=1)
            wfull[zz * 2 + xh] = piece_w
            at_chunk = pl.ds(pl.multiple_of((zz * 2 + xh) * chunk, chunk), chunk)
            acc = (acc[0] + dot(tok[:, at_chunk], piece_w), acc[1] + dot(xsib[:, at_chunk], piece_w))
        return acc

    zero = jnp.zeros((rows, 3 * HEAD), F32)
    acc = lax.fori_loop(0, size["z"], project, (zero, zero))
    for b in range(2):
        proj[b] = acc[b].astype(BF16)

    shrink = 1.0 / HEAD
    def block(b, p):
        return proj[b, :, p * HEAD : (p + 1) * HEAD]

    slices = seqs
    deep = 2 * HEAD // slices

    def exchange(source, target, key):
        index = number(key)

        def send(k, _):
            place = lax.rem(s + k, seqs)
            remote(scan.at[source, place], scan.at[target, s], index, (place, d)).start()
            return 0

        lax.fori_loop(1, seqs, send, 0)
        scan[target, s] = scan[source, s]
        drain(scan.at[target, pl.ds(0, seqs - 1)], recv_sem.at[index])
        drain(scan.at[source, pl.ds(0, seqs - 1)], send_sem.at[index])

    def carry(first_slot, key, backward):
        exchange(first_slot, first_slot + 1, key + "1")

        def step(i, run):
            r = seqs - 1 - i if backward else i
            scan[first_slot + 2, r] = run.astype(BF16)
            return run * keep[r] + scan[first_slot + 1, r].astype(F32)

        lax.fori_loop(0, seqs, step, jnp.zeros((deep, HEAD), F32))
        exchange(first_slot + 2, first_slot + 3, key + "2")
        return scan[first_slot + 3].reshape(2, HEAD, HEAD)

    def give(slot, b, state):
        scan[slot, pl.ds(b * slices // 2, slices // 2)] = state.astype(BF16).reshape(slices // 2, deep, HEAD)

    for b in range(2):
        weak[b] = (mask[b, 0] * (shrink * dot_nt(block(b, 0), block(b, 1)))).astype(BF16)
        tail = (mask[b, 2] * block(b, 1).astype(F32)).astype(BF16)
        give(0, b, dot_tn(tail, block(b, 2)))
        hold[b] = dot(weak[b], block(b, 2))
    incoming = carry(0, "f", False)

    for b in range(2):
        leading = mask[b, 1]
        q, k, v = block(b, 0), block(b, 1), block(b, 2)
        attended = hold[b] + leading * (shrink * dot(q, incoming[b]))
        inverse = lax.rsqrt(jnp.mean(attended * attended, axis=1, keepdims=True) + 1.0)
        result = (attended * inverse).astype(BF16)
        if b == 0:
            kept_n[...] = result
        else:
            nsend[...] = result
        upstream = cots[b].astype(F32)
        mean = jnp.mean(upstream * attended, axis=1, keepdims=True)
        grad = (inverse * upstream - attended * (inverse * inverse * inverse * mean)).astype(BF16)
        head = (leading * q.astype(F32)).astype(BF16)
        give(4, b, dot_tn(head, grad))
        mixed = (mask[b, 0] * (shrink * dot_nt(grad, v))).astype(BF16)
        grad_q = dot(mixed, k) + leading * (shrink * dot_nt(grad, incoming[b]))
        gbuf[b, :, 0:HEAD] = grad_q.astype(BF16)
        held[b, 0] = dot_tn(mixed, q)
        held[b, 1] = dot_tn(weak[b], grad)
    swap_n = remote(nsend, nrecv, number("n"), sibling)
    swap_n.start()
    arriving = carry(4, "r", True)
    for b in range(2):
        trailing = mask[b, 2] * shrink
        grad_k = held[b, 0] + trailing * dot_nt(block(b, 2), arriving[b])
        grad_v = held[b, 1] + trailing * dot(block(b, 1), arriving[b])
        gbuf[b, :, HEAD : 2 * HEAD] = grad_k.astype(BF16)
        gbuf[b, :, 2 * HEAD :] = grad_v.astype(BF16)

    def outer(zz, _):
        for xh in range(2):
            x2 = pl.ds(2 * xh, 2)
            at_chunk = pl.ds(pl.multiple_of((zz * 2 + xh) * chunk, chunk), chunk)
            part = dot(xt[at_chunk, :], gbuf[...].reshape(2 * rows, 3 * HEAD)).astype(BF16)
            parts = [part[:, p * HEAD : (p + 1) * HEAD].reshape(size["y"], 2, ROWS, HEAD) for p in range(3)]
            pg[0][zz, :, x2] = parts[0]
            pg[1][:, x2, zz] = parts[1]
            for xl in range(2):
                pg[2][2 * xh + xl, zz] = parts[2][:, xl]
        return 0

    lax.fori_loop(0, size["z"], outer, 0)

    def inner(i, _):
        at_chunk = pl.ds(pl.multiple_of(i * chunk, chunk), chunk)
        part = dot_nt(gbuf[...].reshape(2 * rows, 3 * HEAD), wfull[i])
        gown[:, at_chunk] = part[:rows]
        gsend[:, at_chunk] = part[rows:].astype(BF16)
        return 0

    lists = []
    for p in range(3):
        steps = size[ORDERS[p][2]] // 2
        for sign in (1, -1):
            far_half = list(half(p, sign))
            hops = [(0, sub) for sub in far_half]
            if steps > 1:
                hops += [(1, sub) for sub in range(subs[p]) if sub not in far_half]
                hops += [(1, sub) for sub in far_half]
            hops += [(k, sub) for k in range(2, steps) for sub in range(subs[p])]
            lists.append((p, sign, hops))
    coming = {}

    def slot(p, sign, k, sub):
        return ring[p].at[0 if sign > 0 else 1, k, piece(p, sub)]

    def add(target, source):
        target[...] = (target[...].astype(F32) + source[...].astype(F32)).astype(BF16)

    turns = max(len(hops) for _, _, hops in lists)
    done = 0
    for turn in range(turns):
        for p, sign, hops in lists:
            if turn >= len(hops):
                continue
            k, sub = hops[turn]
            a3 = ORDERS[p][2]
            steps = size[a3] // 2
            mine = pg[p].at[along(a3, sign * (steps - k)), piece(p, sub)]
            if (p, sign, k - 1, sub) in coming:
                coming[p, sign, k - 1, sub].wait_recv()
                add(mine, slot(p, sign, k - 1, sub))
            copy = remote(mine, slot(p, sign, k, sub), number("r3", p, sign, k, sub), at(a3, along(a3, sign)))
            copy.start()
            coming[p, sign, k, sub] = copy
        upto = min(seqs, -(-seqs * (turn + 1) // (turns - 1)))
        if upto > done:
            lax.fori_loop(done, upto, inner, 0)
            done = upto
    swap_g = remote(gsend, grecv, number("gi"), sibling)
    swap_g.start()
    for p, (a1, a2, a3) in enumerate(ORDERS):
        steps = size[a3] // 2
        for sub in range(subs[p]):
            mine = pg[p].at[me[a3], piece(p, sub)]
            for sign in (1, -1):
                if (p, sign, steps - 1, sub) in coming:
                    coming[p, sign, steps - 1, sub].wait_recv()
            both = [slot(p, sign, steps - 1, sub)[...].astype(F32) for sign in (1, -1) if (p, sign, steps - 1, sub) in coming]
            mine[...] = functools.reduce(lambda a, b: a + b, both, mine[...].astype(F32)).astype(BF16)
        index = number("r2", p)

        def three(k, _, p=p, a2=a2, a3=a3, index=index):
            place = along(a2, k)
            remote(pg[p].at[me[a3], place], far[p].at[me[a2]], index, at(a2, place)).start()
            return 0

        lax.fori_loop(1, size[a2], three, 0)

    swap_n.wait_recv()
    mine, other = kept_n[...].astype(F32), nrecv[...].astype(F32)
    normed[:, :HEAD] = jnp.where(first, mine, other).astype(BF16)
    normed[:, HEAD:] = jnp.where(first, other, mine).astype(BF16)
    for p, (a1, a2, a3) in enumerate(ORDERS):
        drain(far[p].at[pl.ds(0, size[a2] - 1)], recv_sem.at[number("r2", p)])
        mine = pg[p].at[me[a3], me[a2]]
        total = mine[...].astype(F32)
        for k in range(1, size[a2]):
            total = total + far[p][along(a2, k)].astype(F32)
        mine[...] = total.astype(BF16)
        index = number("r1", p)

        def four(k, _, p=p, a1=a1, mine=mine, index=index):
            place = along(a1, k)
            remote(mine.at[place], near[p].at[me[a1]], index, at(a1, place)).start()
            return 0

        lax.fori_loop(1, size[a1], four, 0)

    swap_g.wait_recv()

    def close(i, _):
        at_chunk = pl.ds(pl.multiple_of(i * chunk, chunk), chunk)
        gin[:, at_chunk] = (gown[:, at_chunk] + grecv[:, at_chunk].astype(F32)).astype(BF16)
        return 0

    lax.fori_loop(0, seqs, close, 0)
    factor = 1.0 / math.sqrt(size["y"] * 4 * seqs * rows)
    kept = []
    for p, (a1, a2, a3) in enumerate(ORDERS):
        drain(near[p].at[pl.ds(0, size[a1] - 1)], recv_sem.at[number("r1", p)])
        total = pg[p][me[a3], me[a2], me[a1]].astype(F32)
        for k in range(1, size[a1]):
            total = total + near[p][along(a1, k)].astype(F32)
        total = factor * total
        kept.append(jnp.where(first, total[:8], total[8:]))
        dsend[:, p * HEAD : (p + 1) * HEAD] = jnp.where(first, total[8:], total[:8])
    swap_d = remote(dsend, drecv, number("d"), sibling)
    swap_d.start()
    for copy in coming.values():
        copy.wait_send()
    for p, (a1, a2, a3) in enumerate(ORDERS):
        drain(far[p].at[pl.ds(0, size[a2] - 1)], send_sem.at[number("r2", p)])
        drain(near[p].at[pl.ds(0, size[a1] - 1)], send_sem.at[number("r1", p)])
    swap_n.wait_send()
    swap_g.wait_send()
    swap_d.wait()
    columns = []
    for p in range(3):
        other = drecv[:, p * HEAD : (p + 1) * HEAD]
        columns += [jnp.where(first, kept[p], other), jnp.where(first, other, kept[p])]
    gw[...] = jnp.concatenate(columns, axis=1).astype(BF16)


def solution(mesh):
    seqs, dps = mesh.shape["seq"], mesh.shape["dp"]
    size = {"x": 4, "y": dps // 4, "z": seqs // 2}
    subs = (2, 2, 4)

    def shards(inputs, weights, lengths, cotangent):
        tokens = inputs[0]
        rows, width = tokens.shape
        chunk = width // seqs
        wide = 3 * HEAD
        shapes = []
        for order in ORDERS:
            shapes.append(tuple(size[a] for a in order[::-1]) + (ROWS, HEAD))
        scratch = [
            pltpu.VMEM((rows, width), BF16),
            pltpu.VMEM((width, 2 * rows), BF16),
            pltpu.VMEM((seqs, chunk, wide), BF16),
            pltpu.VMEM((8, wide), F32),
            pltpu.VMEM((8, wide), F32),
            pltpu.VMEM((2, NDOC, 8, HEAD), F32),
            pltpu.VMEM((rows, HEAD), BF16),
            pltpu.VMEM((2, rows, HEAD), BF16),
            pltpu.VMEM((2, rows, wide), BF16),
            pltpu.VMEM((8, seqs, 2 * HEAD // seqs, HEAD), BF16),
            pltpu.VMEM((seqs, 2 * HEAD // seqs, HEAD), F32),
            pltpu.VMEM((2, rows, wide), BF16),
            pltpu.VMEM((2, 3, rows, rows), F32),
            pltpu.VMEM((2, rows, rows), BF16),
            pltpu.VMEM((2, rows, HEAD), F32),
            pltpu.VMEM((2, 2, rows, HEAD), F32),
            pltpu.VMEM((rows, HEAD), BF16),
            pltpu.VMEM((rows, HEAD), BF16),
            pltpu.VMEM((rows, HEAD), BF16),
            pltpu.VMEM((rows, width), F32),
            pltpu.VMEM((rows, width), BF16),
            pltpu.VMEM((rows, width), BF16),
            pltpu.VMEM((8, wide), F32),
            pltpu.VMEM((8, wide), F32),
            pltpu.SemaphoreType.DMA((120,)),
            pltpu.SemaphoreType.DMA((120,)),
        ]
        scratch += [pltpu.VMEM(shape, BF16) for shape in shapes]
        scratch += [pltpu.VMEM(shape, BF16) for shape in shapes]
        scratch += [pltpu.VMEM((2, shape[0] // 2) + shape[1:], BF16) for shape in shapes]
        scratch += [pltpu.VMEM(shape[1:], BF16) for shape in shapes]
        scratch += [pltpu.VMEM(shape[2:], BF16) for shape in shapes]
        vmem = pl.BlockSpec(memory_space=pltpu.VMEM)
        normed, gin, gw = pl.pallas_call(
            functools.partial(kernel, size, subs),
            out_shape=(
                jax.ShapeDtypeStruct((rows, 2 * HEAD), BF16),
                jax.ShapeDtypeStruct((rows, width), BF16),
                jax.ShapeDtypeStruct((8, 2 * wide), BF16),
            ),
            in_specs=[vmem, vmem, pl.BlockSpec(memory_space=pltpu.SMEM), vmem],
            out_specs=(vmem, vmem, vmem),
            scratch_shapes=scratch,
            compiler_params=pltpu.CompilerParams(
                collective_id=0, has_side_effects=True, vmem_limit_bytes=48 * 1024 * 1024
            ),
            cost_estimate=pl.CostEstimate(flops=3 * 10**9, bytes_accessed=4 * 10**6, transcendentals=0),
        )(tokens, weights, lengths, cotangent[0])
        return normed[None], gin[None], gw

    placed = (P("dp", "seq", None), P(("seq", "dp"), None), P("dp", None), P("dp", "seq", None))
    return jax.shard_map(
        shards,
        mesh=mesh,
        in_specs=placed,
        out_specs=(P("dp", "seq", None), P("dp", "seq", None), P(("seq", "dp"), None)),
        check_vma=False,
    )
```

```python
import functools
import math

import jax
import jax.numpy as jnp
from jax import lax
from jax.experimental import pallas as pl
from jax.experimental.pallas import tpu as pltpu
from jax.sharding import PartitionSpec as P

HEAD = 128
NDOC = 8
ROWS = 16
MESH = pl.DeviceIdType.MESH
F32, BF16 = jnp.float32, jnp.bfloat16
ORDERS = (("y", "z", "x"), ("x", "y", "z"), ("x", "z", "y"))


def dot(a, b):
    return jnp.dot(a, b, preferred_element_type=F32)


def dot_nt(a, b):
    return lax.dot_general(a, b, (((1,), (1,)), ((), ())), preferred_element_type=F32)


def dot_tn(a, b):
    return lax.dot_general(a, b, (((0,), (0,)), ((), ())), preferred_element_type=F32)


def kernel(size, tok_hbm, w_hbm, lens_hbm, cot_hbm, normed, gin, gw, *rest):
    (x2, w, cot, lens, xt, wq, wkv, wsend, wrecv, starts, csend, cots, proj, scan, keep, gbuf, mask, weak, hold, held,
     kept_n, nsend, nrecv, gown, gsend, grecv, dsend, drecv, load_sem, send_sem, recv_sem) = rest[:31]
    wg, pg, ring, far, near = (rest[31 + 3 * i : 34 + 3 * i] for i in range(5))
    seqs = 2 * size["z"]
    rows, width = x2.shape[1:]
    chunk = size["y"] * 2 * ROWS
    s, d = lax.axis_index("seq"), lax.axis_index("dp")
    c = lax.rem(d, 2)
    me = {"x": lax.rem(s, 2) * 2 + lax.rem(d // 2, 2), "y": d // 4, "z": s // 2}
    sibling = (s, d + 1 - 2 * c)
    first = c == 0

    def at(axis, place):
        spot = dict(me)
        spot[axis] = place
        return (spot["z"] * 2 + spot["x"] // 2, spot["y"] * 4 + lax.rem(spot["x"], 2) * 2 + c)

    def along(axis, step):
        return lax.rem(me[axis] + step + size[axis], size[axis])

    names, sends = {}, {}

    def remote(src, dst, arrival, departure, target):
        return pltpu.make_async_remote_copy(
            src_ref=src,
            dst_ref=dst,
            send_sem=send_sem.at[sends.setdefault(departure, len(sends))],
            recv_sem=recv_sem.at[names.setdefault(arrival, len(names))],
            device_id=target,
            device_id_type=MESH,
        )

    def arrived(ref, *key):
        pltpu.make_async_copy(ref, ref, recv_sem.at[names[key]]).wait()

    def departed(ref, *key):
        pltpu.make_async_copy(ref, ref, send_sem.at[sends[key]]).wait()

    loads = [
        pltpu.make_async_copy(w_hbm, w, load_sem.at[0]),
        pltpu.make_async_copy(tok_hbm, x2.at[0], load_sem.at[1]),
        pltpu.make_async_copy(lens_hbm, lens, load_sem.at[2]),
        pltpu.make_async_copy(cot_hbm, cot, load_sem.at[3]),
    ]
    for load in loads:
        load.start()

    barrier = pltpu.get_barrier_semaphore()

    def greet(target):
        pl.semaphore_signal(barrier, inc=1, device_id=target, device_id_type=MESH)

    greet(sibling)
    for k in range(1, seqs):
        greet((lax.rem(s + k, seqs), d))
    for k in range(1, size["y"]):
        greet(at("y", along("y", k)))
    greet(at("x", along("x", 1)))
    greet(at("x", along("x", -1)))

    def head_columns(ref, part, mine):
        left = ref[:, part * 2 * HEAD : (2 * part + 1) * HEAD].astype(F32)
        right = ref[:, (2 * part + 1) * HEAD : (2 * part + 2) * HEAD].astype(F32)
        return jnp.where(first == mine, left, right)

    loads[0].wait()
    for p in range(3):
        wsend[:, p * HEAD : (p + 1) * HEAD] = head_columns(w, p, False)

    def turn(b):
        def one(i, _):
            at_chunk = pl.ds(pl.multiple_of(i * chunk, chunk), chunk)
            xt[at_chunk, b * rows : (b + 1) * rows] = x2[b, :, at_chunk].T
            return 0

        return one

    base = (s * rows).astype(F32)
    square = (rows // 8, 8, rows)
    by_row = lax.broadcasted_iota(jnp.int32, square, 0) * 8 + lax.broadcasted_iota(jnp.int32, square, 1)
    by_lane = lax.broadcasted_iota(jnp.int32, square, 2)

    def count(b, positions):
        found = jnp.full(positions.shape, -1.0, F32)
        for i in range(NDOC):
            found = found + jnp.where(starts[b, i][None] <= positions, 1.0, 0.0)
        return found

    def masks(b):
        docs_row = count(b, base + by_row.astype(F32))
        docs_lane = count(b, base + by_lane.astype(F32))
        linked = (docs_row == docs_lane) & (by_lane <= by_row)
        before = count(b, jnp.full((1, 8, HEAD), base - 1.0, F32))
        last = count(b, jnp.full((1, 8, HEAD), base + (rows - 1.0), F32))
        for i, found in enumerate((linked, docs_row == before, docs_row == last)):
            mask[b, i] = jnp.where(found, 1.0, 0.0).reshape(rows, rows)

    pl.semaphore_wait(barrier, 1 + seqs - 1 + size["y"] - 1 + 2)

    swap_w = remote(wsend, wrecv, ("w",), ("w",), sibling)
    swap_s = remote(starts.at[0], starts.at[1], ("s",), ("s",), sibling)
    swap_c = remote(csend, cots.at[1], ("c",), ("c",), sibling)
    swap_x = remote(x2.at[0], x2.at[1], ("x",), ("x",), sibling)
    swap_w.start()

    def offsets(axis):
        n = size[axis]
        return sorted(range(n), key=lambda o: (min(o, n - o), o))

    swap_w.wait_recv()
    for p in (1, 2, 0):
        a1, a2, a3 = ORDERS[p]
        mine = head_columns(w, p, True)
        other = wrecv[:, p * HEAD : (p + 1) * HEAD]
        both = jnp.where(first, jnp.concatenate([mine, other], 0), jnp.concatenate([other, mine], 0))
        wg[p][me[a3], me[a2], me[a1]] = both.astype(BF16)
        block = wg[p].at[me[a3], me[a2], me[a1]]
        for o in offsets(a1)[1:]:
            remote(block, block, ("g1", p), ("g1", p), at(a1, along(a1, o))).start()

    for load in loads[1:]:
        load.wait()
    swap_x.start()
    csend[...] = head_columns(cot, 0, False).astype(BF16)
    swap_c.start()
    cots[0] = head_columns(cot, 0, True).astype(BF16)
    total = jnp.int32(0)
    for i in range(NDOC):
        starts[0, i] = jnp.full((8, HEAD), total.astype(F32))
        total = total + lens[0, i]
    swap_s.start()

    def second(p):
        a1, a2, a3 = ORDERS[p]
        arrived(wg[p].at[0, 0, pl.ds(0, size[a1] - 1)], "g1", p)
        block = wg[p].at[me[a3], me[a2]]
        for o in offsets(a2)[1:]:
            remote(block, block, ("g2", p, size[a2] - o), ("g2", p), at(a2, along(a2, o))).start()

    def halves(axis, sign, order):
        n = size[axis]
        return order[: n // 2] if sign > 0 else order[n // 2 :]

    going, waited, here, turned = {}, set(), set(), {}
    most = size["z"] // 2

    def part_of(sign):
        return pl.ds(0 if sign > 0 else size["y"] // 2, size["y"] // 2)

    def come_round(sign, k):
        if ("z", sign, k) not in here:
            here.add(("z", sign, k))
            turned[sign, k].wait_recv()

    def go_round(k):
        for sign in (1, -1):
            if k:
                come_round(sign, k - 1)
            block = wg[0].at[me["x"], along("z", -sign * k)]
            if k == most - 1:
                block = block.at[part_of(sign)]
            copy = remote(block, block, ("g2", 0, sign, k), ("g2", 0), at("z", along("z", sign)))
            copy.start()
            turned[sign, k] = copy

    def forward(p, sign, k, o):
        a1, a2, a3 = ORDERS[p]
        if p == 0 and k == 0 and o:
            hops = min(o, size[a2] - o)
            for way in (1, -1):
                if hops == most or (o > most) == (way > 0):
                    come_round(way, hops - 1)
        elif k == 0 and o and (p, o) not in here:
            here.add((p, o))
            arrived(wg[p].at[0, 0], "g2", p, o)
        if k > 0:
            going[p, sign, k - 1, o].wait_recv()
            waited.add((p, sign, k - 1, o))
        block = wg[p].at[along(a3, -sign * k), along(a2, o)]
        copy = remote(block, block, ("g3", p, sign, k, o), ("g3", p), at(a3, along(a3, sign)))
        copy.start()
        going[p, sign, k, o] = copy

    def gather_hops(p, sign):
        a1, a2, a3 = ORDERS[p]
        steps, order = size[a3] // 2, offsets(a2)
        return [(k, o) for k in range(steps - 1) for o in order] + [
            (steps - 1, o) for o in halves(a2, sign, order)
        ]

    def gathered(p):
        for key, copy in going.items():
            if key[0] == p and key not in waited:
                copy.wait_recv()

    second(1)
    second(2)
    masks(0)
    lax.fori_loop(0, seqs, turn(0), 0)
    lists = [(p, sign, gather_hops(p, sign)) for p in (1, 2) for sign in (1, -1)]
    for turn_at in range(max(len(hops) for _, _, hops in lists)):
        for p, sign, hops in lists:
            if turn_at < len(hops):
                forward(p, sign, *hops[turn_at])
        if turn_at == 3:
            arrived(wg[0].at[0, 0, pl.ds(0, size["y"] - 1)], "g1", 0)
        if turn_at % 8 == 3:
            go_round(turn_at // 8)
        if turn_at == size["y"] - 1:
            swap_x.wait_recv()
        if turn_at >= size["y"]:
            done = (turn_at - size["y"]) * 2
            if done < seqs:
                lax.fori_loop(done, done + 2, turn(1), 0)

    swap_s.wait_recv()
    masks(1)
    ours = jnp.where(s < seqs // 2, starts[0], starts[1])

    def fill(r, _):
        low = (r * rows).astype(F32)
        inside = jnp.where((ours >= low) & (ours < low + rows), 1.0, 0.0)
        none = 1.0 - jnp.max(inside, axis=0)
        keep[r] = jnp.concatenate([none] * (keep.shape[1] // 8), axis=0)
        return 0

    lax.fori_loop(0, seqs, fill, 0)
    swap_c.wait_recv()
    query_hops = {sign: gather_hops(0, sign) for sign in (1, -1)}
    early = [hop for hop in query_hops[1] if hop[0] == 0]
    for k, o in early:
        for sign in (1, -1):
            forward(0, sign, k, o)
    gathered(1)
    gathered(2)

    def tokens_of(zz):
        at_chunk = pl.ds(pl.multiple_of(zz * 2 * chunk, 2 * chunk), 2 * chunk)
        return x2[:, :, at_chunk].reshape(2 * rows, 2 * chunk)

    def project_kv(zz, acc):
        for xh in range(2):
            pair = pl.ds(2 * xh, 2)
            wkv[zz, xh * chunk : (xh + 1) * chunk, :HEAD] = wg[1][zz, :, pair].reshape(chunk, HEAD)
            wkv[zz, xh * chunk : (xh + 1) * chunk, HEAD:] = wg[2][:, zz, pair].reshape(chunk, HEAD)
        return acc + dot(tokens_of(zz), wkv[zz])

    def project_q(zz, acc):
        for xh in range(2):
            part = jnp.stack([wg[0][2 * xh, zz], wg[0][2 * xh + 1, zz]], axis=1).reshape(chunk, HEAD)
            wq[zz, xh * chunk : (xh + 1) * chunk] = part
        return acc + dot(tokens_of(zz), wq[zz])

    acc = lax.fori_loop(0, size["z"], project_kv, jnp.zeros((2 * rows, 2 * HEAD), F32))
    proj[:, :, HEAD:] = acc.astype(BF16).reshape(2, rows, 2 * HEAD)

    shrink = 1.0 / HEAD

    def block(b, p):
        return proj[b, :, p * HEAD : (p + 1) * HEAD]

    deep = 2 * HEAD // seqs

    def send_slices(source, key):
        def send(i, _):
            k = seqs // 2 + (2 * lax.rem(i, 2) - 1) * ((i + 1) // 2)
            place = lax.rem(s + k, seqs)
            remote(scan.at[source, place], scan.at[source + 1, s], (key,), (key,), (place, d)).start()
            return 0

        lax.fori_loop(0, seqs - 1, send, 0)
        scan[source + 1, s] = scan[source, s]

    def take_slices(source, key):
        arrived(scan.at[source + 1, pl.ds(0, seqs - 1)], key)

    def sweep(source, backward):
        def step(i, run):
            r = seqs - 1 - i if backward else i
            scan[source + 2, r] = run.astype(BF16)
            return run * keep[r] + scan[source + 1, r].astype(F32)

        lax.fori_loop(0, seqs, step, jnp.zeros((deep, HEAD), F32))

    def give(slot, b, state):
        scan[slot, pl.ds(b * seqs // 2, seqs // 2)] = state.astype(BF16).reshape(seqs // 2, deep, HEAD)

    for b in range(2):
        tail = (mask[b, 2] * block(b, 1).astype(F32)).astype(BF16)
        give(0, b, dot_tn(tail, block(b, 2)))
    send_slices(0, "f1")
    for sign in (1, -1):
        for k, o in query_hops[sign][len(early) :]:
            forward(0, sign, k, o)
    take_slices(0, "f1")
    sweep(0, False)
    send_slices(2, "f2")
    gathered(0)
    acc = lax.fori_loop(0, size["z"], project_q, jnp.zeros((2 * rows, HEAD), F32))
    proj[:, :, :HEAD] = acc.astype(BF16).reshape(2, rows, HEAD)
    for b in range(2):
        weak[b] = (mask[b, 0] * (shrink * dot_nt(block(b, 0), block(b, 1)))).astype(BF16)
        hold[b] = dot(weak[b], block(b, 2))
    take_slices(2, "f2")
    def state(slot, b):
        return scan[slot, pl.ds(b * seqs // 2, seqs // 2)].reshape(HEAD, HEAD)

    for b in range(2):
        leading = mask[b, 1]
        q = block(b, 0)
        attended = hold[b] + leading * (shrink * dot(q, state(3, b)))
        inverse = lax.rsqrt(jnp.mean(attended * attended, axis=1, keepdims=True) + 1.0)
        result = (attended * inverse).astype(BF16)
        if b == 0:
            kept_n[...] = result
        else:
            nsend[...] = result
        upstream = cots[b].astype(F32)
        mean = jnp.mean(upstream * attended, axis=1, keepdims=True)
        grad = (inverse * upstream - attended * (inverse * inverse * inverse * mean)).astype(BF16)
        cots[b] = grad
        head = (leading * q.astype(F32)).astype(BF16)
        give(4, b, dot_tn(head, grad))
    send_slices(4, "r1")
    swap_n = remote(nsend, nrecv, ("n",), ("n",), sibling)
    swap_n.start()
    for b in range(2):
        grad = cots[b]
        mixed = (mask[b, 0] * (shrink * dot_nt(grad, block(b, 2)))).astype(BF16)
        grad_q = dot(mixed, block(b, 1)) + mask[b, 1] * (shrink * dot_nt(grad, state(3, b)))
        gbuf[b, :, 0:HEAD] = grad_q.astype(BF16)
        held[b, 0] = dot_tn(mixed, block(b, 0))
        held[b, 1] = dot_tn(weak[b], grad)

    def outer_q(zz, _):
        at_chunk = pl.ds(pl.multiple_of(zz * 2 * chunk, 2 * chunk), 2 * chunk)
        part = dot(xt[at_chunk, :], gbuf[:, :, :HEAD].reshape(2 * rows, HEAD)).astype(BF16)
        part = part.reshape(2, size["y"], 2, ROWS, HEAD)
        for xh in range(2):
            for xl in range(2):
                pg[0][2 * xh + xl, zz] = part[xh, :, xl]
        return 0

    def outer_kv(zz, _):
        at_chunk = pl.ds(pl.multiple_of(zz * 2 * chunk, 2 * chunk), 2 * chunk)
        part = dot(xt[at_chunk, :], gbuf[:, :, HEAD:].reshape(2 * rows, 2 * HEAD)).astype(BF16)
        for xh in range(2):
            pair = pl.ds(2 * xh, 2)
            some = part[xh * chunk : (xh + 1) * chunk]
            pg[1][zz, :, pair] = some[:, :HEAD].reshape(size["y"], 2, ROWS, HEAD)
            pg[2][:, zz, pair] = some[:, HEAD:].reshape(size["y"], 2, ROWS, HEAD)
        return 0

    def inner(i, _):
        at_chunk = pl.ds(pl.multiple_of(i * 2 * chunk, 2 * chunk), 2 * chunk)
        part = dot_nt(gbuf[:, :, :HEAD].reshape(2 * rows, HEAD), wq[i])
        part = part + dot_nt(gbuf[:, :, HEAD:].reshape(2 * rows, 2 * HEAD), wkv[i])
        gown[:, at_chunk] = part[:rows]
        gsend[:, at_chunk] = part[rows:].astype(BF16)
        return 0

    def sum_hops(p, sign):
        a1, a2, a3 = ORDERS[p]
        steps, order = size[a3] // 2, offsets(a2)[::-1]
        some = halves(a2, sign, order)
        hops = [(0, o) for o in some]
        if steps > 1:
            hops += [(1, o) for o in order if o not in some] + [(1, o) for o in some]
        return hops + [(k, o) for k in range(2, steps) for o in order]

    coming = {}

    def slot(p, sign, k, o):
        return ring[p].at[0 if sign > 0 else 1, k, along(ORDERS[p][1], o)]

    def pass_on(p, sign, k, o):
        a1, a2, a3 = ORDERS[p]
        mine = pg[p].at[along(a3, sign * (size[a3] // 2 - k)), along(a2, o)]
        if (p, sign, k - 1, o) in coming:
            coming[p, sign, k - 1, o].wait_recv()
            mine[...] = (mine[...].astype(F32) + slot(p, sign, k - 1, o)[...].astype(F32)).astype(BF16)
        copy = remote(mine, slot(p, sign, k, o), ("r3", p, sign, k, o), ("r3", p), at(a3, along(a3, sign)))
        copy.start()
        coming[p, sign, k, o] = copy

    def settle(p, o):
        a1, a2, a3 = ORDERS[p]
        mine = pg[p].at[me[a3], along(a2, o)]
        total = mine[...].astype(F32)
        for sign in (1, -1):
            key = (p, sign, size[a3] // 2 - 1, o)
            if key in coming:
                coming[key].wait_recv()
                total = total + slot(*key)[...].astype(F32)
        mine[...] = total.astype(BF16)
        if o and p:
            remote(mine, far[p].at[me[a2]], ("r2", p), ("r2", p), at(a2, along(a2, o))).start()

    summing = {}

    def sum_round(k):
        for sign in (1, -1):
            mine = pg[0].at[me["x"], along("z", sign * (most - k))]
            base_slot = 0 if sign > 0 else most
            there = far[0].at[base_slot + k]
            if k:
                summing[sign, k - 1].wait_recv()
                rows_in = part_of(sign) if k == 1 else pl.ds(0, size["y"])
                piece = mine.at[rows_in]
                came = far[0][base_slot + k - 1, rows_in].astype(F32)
                piece[...] = (piece[...].astype(F32) + came).astype(BF16)
            else:
                mine, there = mine.at[part_of(sign)], there.at[part_of(sign)]
            copy = remote(mine, there, ("r2", 0, sign, k), ("r2", 0), at("z", along("z", sign)))
            copy.start()
            summing[sign, k] = copy

    def first_sends(p, total):
        a1, a2, a3 = ORDERS[p]
        mine = pg[p].at[me[a3], me[a2]]
        mine[...] = total.astype(BF16)
        for o in offsets(a1)[:0:-1]:
            place = along(a1, o)
            remote(mine.at[place], near[p].at[me[a1]], ("r1", p), ("r1", p), at(a1, place)).start()

    def sum_end():
        total = pg[0][me["x"], me["z"]].astype(F32)
        for sign in (1, -1):
            summing[sign, most - 1].wait_recv()
            total = total + far[0][(0 if sign > 0 else most) + most - 1].astype(F32)
        first_sends(0, total)

    def settle_second(p):
        a1, a2, a3 = ORDERS[p]
        arrived(far[p].at[pl.ds(0, size[a2] - 1)], "r2", p)
        mine = pg[p].at[me[a3], me[a2]]
        total = mine[...].astype(F32)
        for k in range(1, size[a2]):
            total = total + far[p][along(a2, k)].astype(F32)
        first_sends(p, total)

    lax.fori_loop(0, size["z"], outer_q, 0)
    steps_q = {sign: sum_hops(0, sign) for sign in (1, -1)}
    free = size[ORDERS[0][1]]
    for i in range(free):
        for sign in (1, -1):
            pass_on(0, sign, *steps_q[sign][i])
    take_slices(4, "r1")
    sweep(4, True)
    send_slices(6, "r2s")
    for i in range(free, len(steps_q[1])):
        for sign in (1, -1):
            pass_on(0, sign, *steps_q[sign][i])
    take_slices(6, "r2s")
    for b in range(2):
        trailing = mask[b, 2] * shrink
        grad_k = held[b, 0] + trailing * dot_nt(block(b, 2), state(7, b))
        grad_v = held[b, 1] + trailing * dot(block(b, 1), state(7, b))
        gbuf[b, :, HEAD : 2 * HEAD] = grad_k.astype(BF16)
        gbuf[b, :, 2 * HEAD :] = grad_v.astype(BF16)
    lax.fori_loop(0, size["z"], outer_kv, 0)

    lists = [(p, sign, sum_hops(p, sign)) for p in (1, 2) for sign in (1, -1)]
    turns = max(len(hops) for _, _, hops in lists)
    done = 0
    for turn_at in range(turns):
        for p, sign, hops in lists:
            if turn_at < len(hops):
                pass_on(p, sign, *hops[turn_at])
        upto = min(size["z"], -(-size["z"] * (turn_at + 1) * 4 // (turns * 3)))
        if upto > done:
            lax.fori_loop(done, upto, inner, 0)
            done = upto
        if turn_at == 1:
            for o in offsets(ORDERS[0][1])[::-1]:
                settle(0, o)
        if turn_at % 8 == 1:
            sum_round(turn_at // 8)
    swap_g = remote(gsend, grecv, ("gi",), ("gi",), sibling)
    swap_g.start()
    for o in offsets(ORDERS[1][1])[::-1]:
        settle(1, o)
        settle(2, o)
    sum_end()
    swap_n.wait_recv()
    mine, other = kept_n[...].astype(F32), nrecv[...].astype(F32)
    normed[:, :HEAD] = jnp.where(first, mine, other).astype(BF16)
    normed[:, HEAD:] = jnp.where(first, other, mine).astype(BF16)
    settle_second(1)
    settle_second(2)
    swap_g.wait_recv()

    def close(i, _):
        at_chunk = pl.ds(pl.multiple_of(i * chunk, chunk), chunk)
        gin[:, at_chunk] = (gown[:, at_chunk] + grecv[:, at_chunk].astype(F32)).astype(BF16)
        return 0

    lax.fori_loop(0, seqs, close, 0)
    factor = 1.0 / math.sqrt(size["y"] * 4 * seqs * rows)
    kept = []
    for p, (a1, a2, a3) in enumerate(ORDERS):
        arrived(near[p].at[pl.ds(0, size[a1] - 1)], "r1", p)
        total = pg[p][me[a3], me[a2], me[a1]].astype(F32)
        for k in range(1, size[a1]):
            total = total + near[p][along(a1, k)].astype(F32)
        total = factor * total
        kept.append(jnp.where(first, total[:8], total[8:]))
        dsend[:, p * HEAD : (p + 1) * HEAD] = jnp.where(first, total[8:], total[:8])
    swap_d = remote(dsend, drecv, ("d",), ("d",), sibling)
    swap_d.start()
    for p, (a1, a2, a3) in enumerate(ORDERS):
        departed(wg[p].at[0, 0, pl.ds(0, size[a1] - 1)], "g1", p)
        departed(wg[p].at[0, pl.ds(0, size[a2] - 1)], "g2", p)
        departed(wg[p].at[pl.ds(0, size[a3] - 1)], "g3", p)
        departed(pg[p].at[pl.ds(0, size[a3] - 1)], "r3", p)
        departed(far[p].at[pl.ds(0, size[a2] - 1)], "r2", p)
        departed(near[p].at[pl.ds(0, size[a1] - 1)], "r1", p)
    for i, key in enumerate(("f1", "f2", "r1", "r2s")):
        departed(scan.at[2 * i, pl.ds(0, seqs - 1)], key)
    for copy in (swap_w, swap_x, swap_c, swap_s, swap_n, swap_g):
        copy.wait_send()
    swap_d.wait()
    columns = []
    for p in range(3):
        other = drecv[:, p * HEAD : (p + 1) * HEAD]
        columns += [jnp.where(first, kept[p], other), jnp.where(first, other, kept[p])]
    gw[...] = jnp.concatenate(columns, axis=1).astype(BF16)
    assert len(names) <= recv_sem.shape[0] and len(sends) <= send_sem.shape[0]


def solution(mesh):
    seqs, dps = mesh.shape["seq"], mesh.shape["dp"]
    size = {"x": 4, "y": dps // 4, "z": seqs // 2}

    def shards(inputs, weights, lengths, cotangent):
        tokens = inputs[0]
        rows, width = tokens.shape
        chunk = width // seqs
        wide = 3 * HEAD
        shapes = []
        for order in ORDERS:
            shapes.append(tuple(size[a] for a in order[::-1]) + (ROWS, HEAD))
        scratch = [
            pltpu.VMEM((2, rows, width), BF16),
            pltpu.VMEM((8, 2 * wide), BF16),
            pltpu.VMEM((rows, 2 * HEAD), BF16),
            pltpu.SMEM((1, NDOC), jnp.int32),
            pltpu.VMEM((width, 2 * rows), BF16),
            pltpu.VMEM((seqs // 2, 2 * chunk, HEAD), BF16),
            pltpu.VMEM((seqs // 2, 2 * chunk, 2 * HEAD), BF16),
            pltpu.VMEM((8, wide), F32),
            pltpu.VMEM((8, wide), F32),
            pltpu.VMEM((2, NDOC, 8, HEAD), F32),
            pltpu.VMEM((rows, HEAD), BF16),
            pltpu.VMEM((2, rows, HEAD), BF16),
            pltpu.VMEM((2, rows, wide), BF16),
            pltpu.VMEM((8, seqs, 2 * HEAD // seqs, HEAD), BF16),
            pltpu.VMEM((seqs, 2 * HEAD // seqs, HEAD), F32),
            pltpu.VMEM((2, rows, wide), BF16),
            pltpu.VMEM((2, 3, rows, rows), F32),
            pltpu.VMEM((2, rows, rows), BF16),
            pltpu.VMEM((2, rows, HEAD), F32),
            pltpu.VMEM((2, 2, rows, HEAD), F32),
            pltpu.VMEM((rows, HEAD), BF16),
            pltpu.VMEM((rows, HEAD), BF16),
            pltpu.VMEM((rows, HEAD), BF16),
            pltpu.VMEM((rows, width), F32),
            pltpu.VMEM((rows, width), BF16),
            pltpu.VMEM((rows, width), BF16),
            pltpu.VMEM((8, wide), F32),
            pltpu.VMEM((8, wide), F32),
            pltpu.SemaphoreType.DMA((4,)),
            pltpu.SemaphoreType.DMA((40,)),
            pltpu.SemaphoreType.DMA((352,)),
        ]
        scratch += [pltpu.VMEM(shape, BF16) for shape in shapes]
        scratch += [pltpu.VMEM(shape, BF16) for shape in shapes]
        scratch += [pltpu.VMEM((2, shape[0] // 2) + shape[1:], BF16) for shape in shapes]
        scratch += [pltpu.VMEM(shape[1:], BF16) for shape in shapes]
        scratch += [pltpu.VMEM(shape[2:], BF16) for shape in shapes]
        vmem = pl.BlockSpec(memory_space=pltpu.VMEM)
        normed, gin, gw = pl.pallas_call(
            functools.partial(kernel, size),
            out_shape=(
                jax.ShapeDtypeStruct((rows, 2 * HEAD), BF16),
                jax.ShapeDtypeStruct((rows, width), BF16),
                jax.ShapeDtypeStruct((8, 2 * wide), BF16),
            ),
            in_specs=[pl.BlockSpec(memory_space=pltpu.HBM)] * 4,
            out_specs=(vmem, vmem, vmem),
            scratch_shapes=scratch,
            compiler_params=pltpu.CompilerParams(
                collective_id=0, has_side_effects=True, vmem_limit_bytes=48 * 1024 * 1024
            ),
            cost_estimate=pl.CostEstimate(flops=3 * 10**9, bytes_accessed=4 * 10**6, transcendentals=0),
        )(tokens, weights, lengths, cotangent[0])
        return normed[None], gin[None], gw

    placed = (P("dp", "seq", None), P(("seq", "dp"), None), P("dp", None), P("dp", "seq", None))
    return jax.shard_map(
        shards,
        mesh=mesh,
        in_specs=placed,
        out_specs=(P("dp", "seq", None), P("dp", "seq", None), P(("seq", "dp"), None)),
        check_vma=False,
    )
```

```python
import functools
import math

import jax
import jax.numpy as jnp
from jax import lax
from jax.experimental import pallas as pl
from jax.experimental.pallas import tpu as pltpu
from jax.sharding import PartitionSpec as P

HEAD = 128
NDOC = 8
ROWS = 16
MESH = pl.DeviceIdType.MESH
F32, BF16 = jnp.float32, jnp.bfloat16
ORDERS = (("y", "z", "x"), ("x", "y", "z"), ("x", "z", "y"))


def dot(a, b):
    return jnp.dot(a, b, preferred_element_type=F32)


def dot_nt(a, b):
    return lax.dot_general(a, b, (((1,), (1,)), ((), ())), preferred_element_type=F32)


def dot_tn(a, b):
    return lax.dot_general(a, b, (((0,), (0,)), ((), ())), preferred_element_type=F32)


def kernel(size, tok_hbm, w_hbm, lens_hbm, cot_hbm, normed_hbm, gin_hbm, gw_hbm, *rest):
    (x2, w, cot, lens, xt, wq, wkv, wsend, wrecv, starts, csend, cots, proj, scan, keep, gbuf, mask, weak, hold, held,
     kept_n, nsend, nrecv, gown, gsend, grecv, dsend, drecv, normed, gw, load_sem, send_sem, recv_sem) = rest[:33]
    wg, pg, ring, far, near = (rest[33 + 3 * i : 36 + 3 * i] for i in range(5))
    seqs = 2 * size["z"]
    rows, width = x2.shape[1:]
    chunk = size["y"] * 2 * ROWS
    s, d = lax.axis_index("seq"), lax.axis_index("dp")
    c = lax.rem(d, 2)
    me = {"x": lax.rem(s, 2) * 2 + lax.rem(d // 2, 2), "y": d // 4, "z": s // 2}
    sibling = (s, d + 1 - 2 * c)
    first = c == 0

    def at(axis, place):
        spot = dict(me)
        spot[axis] = place
        return (spot["z"] * 2 + spot["x"] // 2, spot["y"] * 4 + lax.rem(spot["x"], 2) * 2 + c)

    def along(axis, step):
        return lax.rem(me[axis] + step + size[axis], size[axis])

    names, sends = {}, {}

    def remote(src, dst, arrival, departure, target):
        return pltpu.make_async_remote_copy(
            src_ref=src,
            dst_ref=dst,
            send_sem=send_sem.at[sends.setdefault(departure, len(sends))],
            recv_sem=recv_sem.at[names.setdefault(arrival, len(names))],
            device_id=target,
            device_id_type=MESH,
        )

    def arrived(ref, *key):
        pltpu.make_async_copy(ref, ref, recv_sem.at[names[key]]).wait()

    def departed(ref, *key):
        pltpu.make_async_copy(ref, ref, send_sem.at[sends[key]]).wait()

    loads = [
        pltpu.make_async_copy(w_hbm, w, load_sem.at[0]),
        pltpu.make_async_copy(tok_hbm, x2.at[0], load_sem.at[1]),
        pltpu.make_async_copy(lens_hbm, lens, load_sem.at[2]),
        pltpu.make_async_copy(cot_hbm, cot, load_sem.at[3]),
    ]
    for load in loads:
        load.start()

    barrier = pltpu.get_barrier_semaphore()

    def greet(target):
        pl.semaphore_signal(barrier, inc=1, device_id=target, device_id_type=MESH)

    greet(sibling)
    for k in range(1, seqs):
        greet((lax.rem(s + k, seqs), d))
    for k in range(1, size["y"]):
        greet(at("y", along("y", k)))
    greet(at("x", along("x", 1)))
    greet(at("x", along("x", -1)))

    def head_columns(ref, part, mine):
        left = ref[:, part * 2 * HEAD : (2 * part + 1) * HEAD].astype(F32)
        right = ref[:, (2 * part + 1) * HEAD : (2 * part + 2) * HEAD].astype(F32)
        return jnp.where(first == mine, left, right)

    loads[0].wait()
    for p in range(3):
        wsend[:, p * HEAD : (p + 1) * HEAD] = head_columns(w, p, False)

    def turn(b):
        def one(i, _):
            at_chunk = pl.ds(pl.multiple_of(i * chunk, chunk), chunk)
            xt[at_chunk, b * rows : (b + 1) * rows] = x2[b, :, at_chunk].T
            return 0

        return one

    base = (s * rows).astype(F32)
    square = (rows // 8, 8, rows)
    by_row = lax.broadcasted_iota(jnp.int32, square, 0) * 8 + lax.broadcasted_iota(jnp.int32, square, 1)
    by_lane = lax.broadcasted_iota(jnp.int32, square, 2)

    def count(b, positions):
        found = jnp.full(positions.shape, -1.0, F32)
        for i in range(NDOC):
            found = found + jnp.where(starts[b, i][None] <= positions, 1.0, 0.0)
        return found

    def masks(b):
        docs_row = count(b, base + by_row.astype(F32))
        docs_lane = count(b, base + by_lane.astype(F32))
        linked = (docs_row == docs_lane) & (by_lane <= by_row)
        before = count(b, jnp.full((1, 8, HEAD), base - 1.0, F32))
        last = count(b, jnp.full((1, 8, HEAD), base + (rows - 1.0), F32))
        for i, found in enumerate((linked, docs_row == before, docs_row == last)):
            mask[b, i] = jnp.where(found, 1.0, 0.0).reshape(rows, rows)

    pl.semaphore_wait(barrier, 1 + seqs - 1 + size["y"] - 1 + 2)

    swap_w = remote(wsend, wrecv, ("w",), ("w",), sibling)
    swap_s = remote(starts.at[0], starts.at[1], ("s",), ("s",), sibling)
    swap_c = remote(csend, cots.at[1], ("c",), ("c",), sibling)
    swap_x = remote(x2.at[0], x2.at[1], ("x",), ("x",), sibling)
    swap_w.start()

    def offsets(axis):
        n = size[axis]
        return sorted(range(n), key=lambda o: (min(o, n - o), o))

    swap_w.wait_recv()
    for p in (1, 2, 0):
        a1, a2, a3 = ORDERS[p]
        mine = head_columns(w, p, True)
        other = wrecv[:, p * HEAD : (p + 1) * HEAD]
        both = jnp.where(first, jnp.concatenate([mine, other], 0), jnp.concatenate([other, mine], 0))
        wg[p][me[a3], me[a2], me[a1]] = both.astype(BF16)
        block = wg[p].at[me[a3], me[a2], me[a1]]
        for o in offsets(a1)[1:]:
            remote(block, block, ("g1", p), ("g1", p), at(a1, along(a1, o))).start()

    for load in loads[1:]:
        load.wait()
    swap_x.start()
    csend[...] = head_columns(cot, 0, False).astype(BF16)
    swap_c.start()
    cots[0] = head_columns(cot, 0, True).astype(BF16)
    total = jnp.int32(0)
    for i in range(NDOC):
        starts[0, i] = jnp.full((8, HEAD), total.astype(F32))
        total = total + lens[0, i]
    swap_s.start()

    def second(p):
        a1, a2, a3 = ORDERS[p]
        arrived(wg[p].at[0, 0, pl.ds(0, size[a1] - 1)], "g1", p)
        block = wg[p].at[me[a3], me[a2]]
        for o in offsets(a2)[1:]:
            remote(block, block, ("g2", p, size[a2] - o), ("g2", p), at(a2, along(a2, o))).start()

    def halves(axis, sign, order):
        n = size[axis]
        return order[: n // 2] if sign > 0 else order[n // 2 :]

    going, waited, here, turned = {}, set(), set(), {}
    most = size["z"] // 2

    def part_of(sign):
        return pl.ds(0 if sign > 0 else size["y"] // 2, size["y"] // 2)

    def come_round(sign, k):
        if ("z", sign, k) not in here:
            here.add(("z", sign, k))
            turned[sign, k].wait_recv()

    def go_round(k):
        for sign in (1, -1):
            if k:
                come_round(sign, k - 1)
            block = wg[0].at[me["x"], along("z", -sign * k)]
            if k == most - 1:
                block = block.at[part_of(sign)]
            copy = remote(block, block, ("g2", 0, sign, k), ("g2", 0), at("z", along("z", sign)))
            copy.start()
            turned[sign, k] = copy

    def forward(p, sign, k, o):
        a1, a2, a3 = ORDERS[p]
        if p == 0 and k == 0 and o:
            hops = min(o, size[a2] - o)
            for way in (1, -1):
                if hops == most or (o > most) == (way > 0):
                    come_round(way, hops - 1)
        elif k == 0 and o and (p, o) not in here:
            here.add((p, o))
            arrived(wg[p].at[0, 0], "g2", p, o)
        if k > 0:
            going[p, sign, k - 1, o].wait_recv()
            waited.add((p, sign, k - 1, o))
        block = wg[p].at[along(a3, -sign * k), along(a2, o)]
        copy = remote(block, block, ("g3", p, sign, k, o), ("g3", p), at(a3, along(a3, sign)))
        copy.start()
        going[p, sign, k, o] = copy

    def gather_hops(p, sign):
        a1, a2, a3 = ORDERS[p]
        steps, order = size[a3] // 2, offsets(a2)
        return [(k, o) for k in range(steps - 1) for o in order] + [
            (steps - 1, o) for o in halves(a2, sign, order)
        ]

    def gathered(p):
        for key, copy in going.items():
            if key[0] == p and key not in waited:
                copy.wait_recv()

    second(1)
    second(2)
    masks(0)
    lax.fori_loop(0, seqs, turn(0), 0)
    query_order = offsets(ORDERS[0][1])
    lists = [(p, sign, gather_hops(p, sign)) for p in (1, 2) for sign in (1, -1)]
    for turn_at in range(max(len(hops) for _, _, hops in lists)):
        for p, sign, hops in lists:
            if turn_at < len(hops):
                forward(p, sign, *hops[turn_at])
        if turn_at == 3:
            arrived(wg[0].at[0, 0, pl.ds(0, size["y"] - 1)], "g1", 0)
        if turn_at % 8 == 3:
            go_round(turn_at // 8)
        if turn_at % 8 == 5 and turn_at > 8:
            third = turn_at // 8
            for o in query_order[2 * third - 1 - (third == 1) : 2 * third + 1]:
                for sign in (1, -1):
                    forward(0, sign, 0, o)
        if turn_at == size["y"] - 1:
            swap_x.wait_recv()
        if turn_at >= size["y"]:
            done = (turn_at - size["y"]) * 2
            if done < seqs:
                lax.fori_loop(done, done + 2, turn(1), 0)

    swap_s.wait_recv()
    masks(1)
    ours = jnp.where(s < seqs // 2, starts[0], starts[1])

    def fill(r, _):
        low = (r * rows).astype(F32)
        inside = jnp.where((ours >= low) & (ours < low + rows), 1.0, 0.0)
        none = 1.0 - jnp.max(inside, axis=0)
        keep[r] = jnp.concatenate([none] * (keep.shape[1] // 8), axis=0)
        return 0

    lax.fori_loop(0, seqs, fill, 0)
    swap_c.wait_recv()
    query_last = {sign: halves(ORDERS[0][1], sign, query_order) for sign in (1, -1)}
    for o in query_order[5:-1]:
        for sign in (1, -1):
            forward(0, sign, 0, o)
    for o in query_last[1][:-1]:
        forward(0, 1, 1, o)
    gathered(1)
    gathered(2)
    for sign in (1, -1):
        forward(0, sign, 0, query_order[-1])

    def tokens_of(zz):
        at_chunk = pl.ds(pl.multiple_of(zz * 2 * chunk, 2 * chunk), 2 * chunk)
        return x2[:, :, at_chunk].reshape(2 * rows, 2 * chunk)

    def project_kv(zz, acc):
        for xh in range(2):
            pair = pl.ds(2 * xh, 2)
            wkv[zz, xh * chunk : (xh + 1) * chunk, :HEAD] = wg[1][zz, :, pair].reshape(chunk, HEAD)
            wkv[zz, xh * chunk : (xh + 1) * chunk, HEAD:] = wg[2][:, zz, pair].reshape(chunk, HEAD)
        return acc + dot(tokens_of(zz), wkv[zz])

    def project_q(zz, acc):
        for xh in range(2):
            part = jnp.stack([wg[0][2 * xh, zz], wg[0][2 * xh + 1, zz]], axis=1).reshape(chunk, HEAD)
            wq[zz, xh * chunk : (xh + 1) * chunk] = part
        return acc + dot(tokens_of(zz), wq[zz])

    acc = lax.fori_loop(0, size["z"], project_kv, jnp.zeros((2 * rows, 2 * HEAD), F32))
    proj[:, :, HEAD:] = acc.astype(BF16).reshape(2, rows, 2 * HEAD)

    shrink = 1.0 / HEAD

    def block(b, p):
        return proj[b, :, p * HEAD : (p + 1) * HEAD]

    deep = 2 * HEAD // seqs

    def send_slices(source, key):
        def send(i, _):
            k = seqs // 2 + (2 * lax.rem(i, 2) - 1) * ((i + 1) // 2)
            place = lax.rem(s + k, seqs)
            remote(scan.at[source, place], scan.at[source + 1, s], (key,), (key,), (place, d)).start()
            return 0

        lax.fori_loop(0, seqs - 1, send, 0)
        scan[source + 1, s] = scan[source, s]

    def take_slices(source, key):
        arrived(scan.at[source + 1, pl.ds(0, seqs - 1)], key)

    def sweep(source, backward):
        def step(i, run):
            r = seqs - 1 - i if backward else i
            scan[source + 2, r] = run.astype(BF16)
            return run * keep[r] + scan[source + 1, r].astype(F32)

        lax.fori_loop(0, seqs, step, jnp.zeros((deep, HEAD), F32))

    def give(slot, b, state):
        scan[slot, pl.ds(b * seqs // 2, seqs // 2)] = state.astype(BF16).reshape(seqs // 2, deep, HEAD)

    for b in range(2):
        tail = (mask[b, 2] * block(b, 1).astype(F32)).astype(BF16)
        give(0, b, dot_tn(tail, block(b, 2)))
    send_slices(0, "f1")
    forward(0, 1, 1, query_last[1][-1])
    for o in query_last[-1]:
        forward(0, -1, 1, o)
    take_slices(0, "f1")
    sweep(0, False)
    send_slices(2, "f2")
    gathered(0)
    acc = lax.fori_loop(0, size["z"], project_q, jnp.zeros((2 * rows, HEAD), F32))
    proj[:, :, :HEAD] = acc.astype(BF16).reshape(2, rows, HEAD)
    for b in range(2):
        weak[b] = (mask[b, 0] * (shrink * dot_nt(block(b, 0), block(b, 1)))).astype(BF16)
        hold[b] = dot(weak[b], block(b, 2))
    take_slices(2, "f2")
    def state(slot, b):
        return scan[slot, pl.ds(b * seqs // 2, seqs // 2)].reshape(HEAD, HEAD)

    for b in range(2):
        leading = mask[b, 1]
        q = block(b, 0)
        attended = hold[b] + leading * (shrink * dot(q, state(3, b)))
        inverse = lax.rsqrt(jnp.mean(attended * attended, axis=1, keepdims=True) + 1.0)
        result = (attended * inverse).astype(BF16)
        if b == 0:
            kept_n[...] = result
        else:
            nsend[...] = result
        upstream = cots[b].astype(F32)
        mean = jnp.mean(upstream * attended, axis=1, keepdims=True)
        grad = (inverse * upstream - attended * (inverse * inverse * inverse * mean)).astype(BF16)
        cots[b] = grad
        head = (leading * q.astype(F32)).astype(BF16)
        give(4, b, dot_tn(head, grad))
    send_slices(4, "r1")
    swap_n = remote(nsend, nrecv, ("n",), ("n",), sibling)
    swap_n.start()
    for b in range(2):
        grad = cots[b]
        mixed = (mask[b, 0] * (shrink * dot_nt(grad, block(b, 2)))).astype(BF16)
        grad_q = dot(mixed, block(b, 1)) + mask[b, 1] * (shrink * dot_nt(grad, state(3, b)))
        gbuf[b, :, 0:HEAD] = grad_q.astype(BF16)
        held[b, 0] = dot_tn(mixed, block(b, 0))
        held[b, 1] = dot_tn(weak[b], grad)

    def outer_q(zz, _):
        at_chunk = pl.ds(pl.multiple_of(zz * 2 * chunk, 2 * chunk), 2 * chunk)
        part = dot(xt[at_chunk, :], gbuf[:, :, :HEAD].reshape(2 * rows, HEAD)).astype(BF16)
        part = part.reshape(2, size["y"], 2, ROWS, HEAD)
        for xh in range(2):
            for xl in range(2):
                pg[0][2 * xh + xl, zz] = part[xh, :, xl]
        return 0

    def outer_kv(zz, _):
        at_chunk = pl.ds(pl.multiple_of(zz * 2 * chunk, 2 * chunk), 2 * chunk)
        part = dot(xt[at_chunk, :], gbuf[:, :, HEAD:].reshape(2 * rows, 2 * HEAD)).astype(BF16)
        for xh in range(2):
            pair = pl.ds(2 * xh, 2)
            some = part[xh * chunk : (xh + 1) * chunk]
            pg[1][zz, :, pair] = some[:, :HEAD].reshape(size["y"], 2, ROWS, HEAD)
            pg[2][:, zz, pair] = some[:, HEAD:].reshape(size["y"], 2, ROWS, HEAD)
        return 0

    def inner(i, _):
        at_chunk = pl.ds(pl.multiple_of(i * 2 * chunk, 2 * chunk), 2 * chunk)
        part = dot_nt(gbuf[:, :, :HEAD].reshape(2 * rows, HEAD), wq[i])
        part = part + dot_nt(gbuf[:, :, HEAD:].reshape(2 * rows, 2 * HEAD), wkv[i])
        gown[:, at_chunk] = part[:rows]
        gsend[:, at_chunk] = part[rows:].astype(BF16)
        return 0

    def sum_hops(p, sign):
        a1, a2, a3 = ORDERS[p]
        steps, order = size[a3] // 2, offsets(a2)[::-1]
        some = halves(a2, sign, order)
        hops = [(0, o) for o in some]
        if steps > 1:
            hops += [(1, o) for o in order if o not in some] + [(1, o) for o in some]
        return hops + [(k, o) for k in range(2, steps) for o in order]

    coming = {}

    def slot(p, sign, k, o):
        return ring[p].at[0 if sign > 0 else 1, k, along(ORDERS[p][1], o)]

    def pass_on(p, sign, k, o):
        a1, a2, a3 = ORDERS[p]
        mine = pg[p].at[along(a3, sign * (size[a3] // 2 - k)), along(a2, o)]
        if (p, sign, k - 1, o) in coming:
            coming[p, sign, k - 1, o].wait_recv()
            mine[...] = (mine[...].astype(F32) + slot(p, sign, k - 1, o)[...].astype(F32)).astype(BF16)
        copy = remote(mine, slot(p, sign, k, o), ("r3", p, sign, k, o), ("r3", p), at(a3, along(a3, sign)))
        copy.start()
        coming[p, sign, k, o] = copy

    def settle(p, o):
        a1, a2, a3 = ORDERS[p]
        mine = pg[p].at[me[a3], along(a2, o)]
        total = mine[...].astype(F32)
        for sign in (1, -1):
            key = (p, sign, size[a3] // 2 - 1, o)
            if key in coming:
                coming[key].wait_recv()
                total = total + slot(*key)[...].astype(F32)
        mine[...] = total.astype(BF16)
        if o and p:
            remote(mine, far[p].at[me[a2]], ("r2", p), ("r2", p), at(a2, along(a2, o))).start()

    summing = {}

    def sum_round(k):
        for sign in (1, -1):
            mine = pg[0].at[me["x"], along("z", sign * (most - k))]
            base_slot = 0 if sign > 0 else most
            there = far[0].at[base_slot + k]
            if k:
                summing[sign, k - 1].wait_recv()
                rows_in = part_of(sign) if k == 1 else pl.ds(0, size["y"])
                piece = mine.at[rows_in]
                came = far[0][base_slot + k - 1, rows_in].astype(F32)
                piece[...] = (piece[...].astype(F32) + came).astype(BF16)
            else:
                mine, there = mine.at[part_of(sign)], there.at[part_of(sign)]
            copy = remote(mine, there, ("r2", 0, sign, k), ("r2", 0), at("z", along("z", sign)))
            copy.start()
            summing[sign, k] = copy

    def first_sends(p, total):
        a1, a2, a3 = ORDERS[p]
        mine = pg[p].at[me[a3], me[a2]]
        mine[...] = total.astype(BF16)
        for o in offsets(a1)[:0:-1]:
            place = along(a1, o)
            remote(mine.at[place], near[p].at[me[a1]], ("r1", p), ("r1", p), at(a1, place)).start()

    def sum_end():
        total = pg[0][me["x"], me["z"]].astype(F32)
        for sign in (1, -1):
            summing[sign, most - 1].wait_recv()
            total = total + far[0][(0 if sign > 0 else most) + most - 1].astype(F32)
        first_sends(0, total)

    def settle_second(p):
        a1, a2, a3 = ORDERS[p]
        arrived(far[p].at[pl.ds(0, size[a2] - 1)], "r2", p)
        mine = pg[p].at[me[a3], me[a2]]
        total = mine[...].astype(F32)
        for k in range(1, size[a2]):
            total = total + far[p][along(a2, k)].astype(F32)
        first_sends(p, total)

    lax.fori_loop(0, size["z"], outer_q, 0)
    steps_q = {sign: sum_hops(0, sign) for sign in (1, -1)}
    free = size[ORDERS[0][1]]
    for i in range(free):
        for sign in (1, -1):
            pass_on(0, sign, *steps_q[sign][i])
    take_slices(4, "r1")
    sweep(4, True)
    send_slices(6, "r2s")
    for i in range(free, len(steps_q[1])):
        for sign in (1, -1):
            pass_on(0, sign, *steps_q[sign][i])
    take_slices(6, "r2s")
    for b in range(2):
        trailing = mask[b, 2] * shrink
        grad_k = held[b, 0] + trailing * dot_nt(block(b, 2), state(7, b))
        grad_v = held[b, 1] + trailing * dot(block(b, 1), state(7, b))
        gbuf[b, :, HEAD : 2 * HEAD] = grad_k.astype(BF16)
        gbuf[b, :, 2 * HEAD :] = grad_v.astype(BF16)
    lax.fori_loop(0, size["z"], outer_kv, 0)

    lists = [(p, sign, sum_hops(p, sign)) for p in (1, 2) for sign in (1, -1)]
    turns = max(len(hops) for _, _, hops in lists)
    done = 0
    for turn_at in range(turns):
        for p, sign, hops in lists:
            if turn_at < len(hops):
                pass_on(p, sign, *hops[turn_at])
        upto = min(size["z"], -(-size["z"] * (turn_at + 1) * 4 // (turns * 3)))
        if upto > done:
            lax.fori_loop(done, upto, inner, 0)
            done = upto
        if turn_at == 1:
            for o in offsets(ORDERS[0][1])[::-1]:
                settle(0, o)
        if turn_at % 8 == 1:
            sum_round(turn_at // 8)
    swap_g = remote(gsend, grecv, ("gi",), ("gi",), sibling)
    swap_g.start()
    for o in offsets(ORDERS[1][1])[::-1]:
        settle(1, o)
        settle(2, o)
    sum_end()
    swap_n.wait_recv()
    mine, other = kept_n[...].astype(F32), nrecv[...].astype(F32)
    normed[:, :HEAD] = jnp.where(first, mine, other).astype(BF16)
    normed[:, HEAD:] = jnp.where(first, other, mine).astype(BF16)
    stores = [pltpu.make_async_copy(normed, normed_hbm, load_sem.at[4])]
    stores[0].start()
    settle_second(1)
    settle_second(2)
    swap_g.wait_recv()

    def close(i, _):
        at_chunk = pl.ds(pl.multiple_of(i * chunk, chunk), chunk)
        grecv[:, at_chunk] = (gown[:, at_chunk] + grecv[:, at_chunk].astype(F32)).astype(BF16)
        return 0

    lax.fori_loop(0, seqs, close, 0)
    stores.append(pltpu.make_async_copy(grecv, gin_hbm, load_sem.at[5]))
    stores[1].start()
    factor = 1.0 / math.sqrt(size["y"] * 4 * seqs * rows)
    kept = []
    for p, (a1, a2, a3) in enumerate(ORDERS):
        arrived(near[p].at[pl.ds(0, size[a1] - 1)], "r1", p)
        total = pg[p][me[a3], me[a2], me[a1]].astype(F32)
        for k in range(1, size[a1]):
            total = total + near[p][along(a1, k)].astype(F32)
        total = factor * total
        kept.append(jnp.where(first, total[:8], total[8:]))
        dsend[:, p * HEAD : (p + 1) * HEAD] = jnp.where(first, total[8:], total[:8])
    swap_d = remote(dsend, drecv, ("d",), ("d",), sibling)
    swap_d.start()
    for p, (a1, a2, a3) in enumerate(ORDERS):
        departed(wg[p].at[0, 0, pl.ds(0, size[a1] - 1)], "g1", p)
        departed(wg[p].at[0, pl.ds(0, size[a2] - 1)], "g2", p)
        departed(wg[p].at[pl.ds(0, size[a3] - 1)], "g3", p)
        departed(pg[p].at[pl.ds(0, size[a3] - 1)], "r3", p)
        departed(far[p].at[pl.ds(0, size[a2] - 1)], "r2", p)
        departed(near[p].at[pl.ds(0, size[a1] - 1)], "r1", p)
    for i, key in enumerate(("f1", "f2", "r1", "r2s")):
        departed(scan.at[2 * i, pl.ds(0, seqs - 1)], key)
    for copy in (swap_w, swap_x, swap_c, swap_s, swap_n, swap_g):
        copy.wait_send()
    swap_d.wait()
    columns = []
    for p in range(3):
        other = drecv[:, p * HEAD : (p + 1) * HEAD]
        columns += [jnp.where(first, kept[p], other), jnp.where(first, other, kept[p])]
    gw[...] = jnp.concatenate(columns, axis=1).astype(BF16)
    stores.append(pltpu.make_async_copy(gw, gw_hbm, load_sem.at[6]))
    stores[2].start()
    for store in stores:
        store.wait()
    assert len(names) <= recv_sem.shape[0] and len(sends) <= send_sem.shape[0]


def deliver(normed, gin, gw, normed_out, gin_out, gw_out, sem):
    parts = 4
    span = gin.shape[0] // parts
    copies = [pltpu.make_async_copy(normed, normed_out, sem.at[0]), pltpu.make_async_copy(gw, gw_out, sem.at[1])]
    for i in range(parts):
        rows = pl.ds(i * span, span)
        copies.append(pltpu.make_async_copy(gin.at[rows], gin_out.at[rows], sem.at[2 + i]))
    for copy in copies:
        copy.start()
    for copy in copies:
        copy.wait()


def solution(mesh):
    seqs, dps = mesh.shape["seq"], mesh.shape["dp"]
    size = {"x": 4, "y": dps // 4, "z": seqs // 2}

    def shards(inputs, weights, lengths, cotangent):
        tokens = inputs[0]
        rows, width = tokens.shape
        chunk = width // seqs
        wide = 3 * HEAD
        shapes = []
        for order in ORDERS:
            shapes.append(tuple(size[a] for a in order[::-1]) + (ROWS, HEAD))
        scratch = [
            pltpu.VMEM((2, rows, width), BF16),
            pltpu.VMEM((8, 2 * wide), BF16),
            pltpu.VMEM((rows, 2 * HEAD), BF16),
            pltpu.SMEM((1, NDOC), jnp.int32),
            pltpu.VMEM((width, 2 * rows), BF16),
            pltpu.VMEM((seqs // 2, 2 * chunk, HEAD), BF16),
            pltpu.VMEM((seqs // 2, 2 * chunk, 2 * HEAD), BF16),
            pltpu.VMEM((8, wide), F32),
            pltpu.VMEM((8, wide), F32),
            pltpu.VMEM((2, NDOC, 8, HEAD), F32),
            pltpu.VMEM((rows, HEAD), BF16),
            pltpu.VMEM((2, rows, HEAD), BF16),
            pltpu.VMEM((2, rows, wide), BF16),
            pltpu.VMEM((8, seqs, 2 * HEAD // seqs, HEAD), BF16),
            pltpu.VMEM((seqs, 2 * HEAD // seqs, HEAD), F32),
            pltpu.VMEM((2, rows, wide), BF16),
            pltpu.VMEM((2, 3, rows, rows), F32),
            pltpu.VMEM((2, rows, rows), BF16),
            pltpu.VMEM((2, rows, HEAD), F32),
            pltpu.VMEM((2, 2, rows, HEAD), F32),
            pltpu.VMEM((rows, HEAD), BF16),
            pltpu.VMEM((rows, HEAD), BF16),
            pltpu.VMEM((rows, HEAD), BF16),
            pltpu.VMEM((rows, width), F32),
            pltpu.VMEM((rows, width), BF16),
            pltpu.VMEM((rows, width), BF16),
            pltpu.VMEM((8, wide), F32),
            pltpu.VMEM((8, wide), F32),
            pltpu.VMEM((rows, 2 * HEAD), BF16),
            pltpu.VMEM((8, 2 * wide), BF16),
            pltpu.SemaphoreType.DMA((7,)),
            pltpu.SemaphoreType.DMA((29,)),
            pltpu.SemaphoreType.DMA((321,)),
        ]
        scratch += [pltpu.VMEM(shape, BF16) for shape in shapes]
        scratch += [pltpu.VMEM(shape, BF16) for shape in shapes]
        scratch += [pltpu.VMEM((2, shape[0] // 2) + shape[1:], BF16) for shape in shapes]
        scratch += [pltpu.VMEM(shape[1:], BF16) for shape in shapes]
        scratch += [pltpu.VMEM(shape[2:], BF16) for shape in shapes]
        hbm = pl.BlockSpec(memory_space=pltpu.HBM)
        results = (
            jax.ShapeDtypeStruct((rows, 2 * HEAD), BF16),
            jax.ShapeDtypeStruct((rows, width), BF16),
            jax.ShapeDtypeStruct((8, 2 * wide), BF16),
        )
        found = pl.pallas_call(
            functools.partial(kernel, size),
            out_shape=results,
            in_specs=[hbm] * 4,
            out_specs=(hbm, hbm, hbm),
            scratch_shapes=scratch,
            compiler_params=pltpu.CompilerParams(
                collective_id=0, has_side_effects=True, vmem_limit_bytes=56 * 1024 * 1024
            ),
            cost_estimate=pl.CostEstimate(flops=3 * 10**9, bytes_accessed=4 * 10**6, transcendentals=0),
        )(tokens, weights, lengths, cotangent[0])
        normed, gin, gw = pl.pallas_call(
            deliver,
            out_shape=results,
            in_specs=[pl.BlockSpec(memory_space=pltpu.VMEM)] * 3,
            out_specs=(hbm, hbm, hbm),
            scratch_shapes=[pltpu.SemaphoreType.DMA((6,))],
        )(*found)
        return normed[None], gin[None], gw

    placed = (P("dp", "seq", None), P(("seq", "dp"), None), P("dp", None), P("dp", "seq", None))
    return jax.shard_map(
        shards,
        mesh=mesh,
        in_specs=placed,
        out_specs=(P("dp", "seq", None), P("dp", "seq", None), P(("seq", "dp"), None)),
        check_vma=False,
    )
```

```python
import functools
import math

import jax
import jax.numpy as jnp
from jax import lax
from jax.experimental import pallas as pl
from jax.experimental.pallas import tpu as pltpu
from jax.sharding import PartitionSpec as P

HEAD = 128
NDOC = 8
ROWS = 16
MESH = pl.DeviceIdType.MESH
F32, BF16 = jnp.float32, jnp.bfloat16
ORDERS = (("y", "z", "x"), ("x", "y", "z"), ("x", "z", "y"))


def dot(a, b):
    return jnp.dot(a, b, preferred_element_type=F32)


def dot_nt(a, b):
    return lax.dot_general(a, b, (((1,), (1,)), ((), ())), preferred_element_type=F32)


def dot_tn(a, b):
    return lax.dot_general(a, b, (((0,), (0,)), ((), ())), preferred_element_type=F32)


def kernel(size, tok_hbm, w_hbm, lens_hbm, cot_hbm, normed_hbm, gin_hbm, gw_hbm, *rest):
    (x2, w, cot, lens, xt, wq, wkv, wsend, wrecv, starts, csend, cots, proj, scan, keep, gbuf, mask, weak, hold, held,
     kept_n, nsend, nrecv, gown, gsend, grecv, dsend, drecv, normed, gw, load_sem, send_sem, recv_sem) = rest[:33]
    wg, pg, ring, far, near = (rest[33 + 3 * i : 36 + 3 * i] for i in range(5))
    seqs = 2 * size["z"]
    rows, width = x2.shape[1:]
    chunk = size["y"] * 2 * ROWS
    s, d = lax.axis_index("seq"), lax.axis_index("dp")
    c = lax.rem(d, 2)
    me = {"x": lax.rem(s, 2) * 2 + lax.rem(d // 2, 2), "y": d // 4, "z": s // 2}
    sibling = (s, d + 1 - 2 * c)
    first = c == 0

    def at(axis, place):
        spot = dict(me)
        spot[axis] = place
        return (spot["z"] * 2 + spot["x"] // 2, spot["y"] * 4 + lax.rem(spot["x"], 2) * 2 + c)

    def along(axis, step):
        return lax.rem(me[axis] + step + size[axis], size[axis])

    names, sends = {}, {}

    def remote(src, dst, arrival, departure, target):
        return pltpu.make_async_remote_copy(
            src_ref=src,
            dst_ref=dst,
            send_sem=send_sem.at[sends.setdefault(departure, len(sends))],
            recv_sem=recv_sem.at[names.setdefault(arrival, len(names))],
            device_id=target,
            device_id_type=MESH,
        )

    def arrived(ref, *key):
        pltpu.make_async_copy(ref, ref, recv_sem.at[names[key]]).wait()

    def departed(ref, *key):
        pltpu.make_async_copy(ref, ref, send_sem.at[sends[key]]).wait()

    loads = [
        pltpu.make_async_copy(w_hbm, w, load_sem.at[0]),
        pltpu.make_async_copy(tok_hbm, x2.at[0], load_sem.at[1]),
        pltpu.make_async_copy(lens_hbm, lens, load_sem.at[2]),
        pltpu.make_async_copy(cot_hbm, cot, load_sem.at[3]),
    ]
    for load in loads:
        load.start()

    barrier = pltpu.get_barrier_semaphore()

    def greet(target):
        pl.semaphore_signal(barrier, inc=1, device_id=target, device_id_type=MESH)

    greet(sibling)
    for k in range(1, seqs):
        greet((lax.rem(s + k, seqs), d))
    for k in range(1, size["y"]):
        greet(at("y", along("y", k)))
    greet(at("x", along("x", 1)))
    greet(at("x", along("x", -1)))

    def head_columns(ref, part, mine):
        left = ref[:, part * 2 * HEAD : (2 * part + 1) * HEAD].astype(F32)
        right = ref[:, (2 * part + 1) * HEAD : (2 * part + 2) * HEAD].astype(F32)
        return jnp.where(first == mine, left, right)

    loads[0].wait()
    for p in range(3):
        wsend[:, p * HEAD : (p + 1) * HEAD] = head_columns(w, p, False)

    def turn(b):
        def one(i, _):
            at_chunk = pl.ds(pl.multiple_of(i * chunk, chunk), chunk)
            xt[at_chunk, b * rows : (b + 1) * rows] = x2[b, :, at_chunk].T
            return 0

        return one

    base = (s * rows).astype(F32)
    square = (rows // 8, 8, rows)
    by_row = lax.broadcasted_iota(jnp.int32, square, 0) * 8 + lax.broadcasted_iota(jnp.int32, square, 1)
    by_lane = lax.broadcasted_iota(jnp.int32, square, 2)

    def count(b, positions):
        found = jnp.full(positions.shape, -1.0, F32)
        for i in range(NDOC):
            found = found + jnp.where(starts[b, i][None] <= positions, 1.0, 0.0)
        return found

    def masks(b):
        docs_row = count(b, base + by_row.astype(F32))
        docs_lane = count(b, base + by_lane.astype(F32))
        linked = (docs_row == docs_lane) & (by_lane <= by_row)
        before = count(b, jnp.full((1, 8, HEAD), base - 1.0, F32))
        last = count(b, jnp.full((1, 8, HEAD), base + (rows - 1.0), F32))
        for i, found in enumerate((linked, docs_row == before, docs_row == last)):
            mask[b, i] = jnp.where(found, 1.0, 0.0).reshape(rows, rows)

    pl.semaphore_wait(barrier, 1 + seqs - 1 + size["y"] - 1 + 2)

    swap_w = remote(wsend, wrecv, ("w",), ("w",), sibling)
    swap_s = remote(starts.at[0], starts.at[1], ("s",), ("s",), sibling)
    swap_c = remote(csend, cots.at[1], ("c",), ("c",), sibling)
    swap_x = remote(x2.at[0], x2.at[1], ("x",), ("x",), sibling)
    swap_w.start()

    def offsets(axis):
        n = size[axis]
        return sorted(range(n), key=lambda o: (min(o, n - o), o))

    swap_w.wait_recv()
    for p in (1, 2, 0):
        a1, a2, a3 = ORDERS[p]
        mine = head_columns(w, p, True)
        other = wrecv[:, p * HEAD : (p + 1) * HEAD]
        both = jnp.where(first, jnp.concatenate([mine, other], 0), jnp.concatenate([other, mine], 0))
        wg[p][me[a3], me[a2], me[a1]] = both.astype(BF16)
        block = wg[p].at[me[a3], me[a2], me[a1]]
        for o in offsets(a1)[1:]:
            remote(block, block, ("g1", p), ("g1", p), at(a1, along(a1, o))).start()

    for load in loads[1:]:
        load.wait()
    swap_x.start()
    csend[...] = head_columns(cot, 0, False).astype(BF16)
    swap_c.start()
    cots[0] = head_columns(cot, 0, True).astype(BF16)
    total = jnp.int32(0)
    for i in range(NDOC):
        starts[0, i] = jnp.full((8, HEAD), total.astype(F32))
        total = total + lens[0, i]
    swap_s.start()

    def second(p):
        a1, a2, a3 = ORDERS[p]
        arrived(wg[p].at[0, 0, pl.ds(0, size[a1] - 1)], "g1", p)
        block = wg[p].at[me[a3], me[a2]]
        for o in offsets(a2)[1:]:
            remote(block, block, ("g2", p, size[a2] - o), ("g2", p), at(a2, along(a2, o))).start()

    def halves(axis, sign, order):
        n = size[axis]
        return order[: n // 2] if sign > 0 else order[n // 2 :]

    going, waited, here, turned = {}, set(), set(), {}
    most = size["z"] // 2

    def part_of(sign):
        return pl.ds(0 if sign > 0 else size["y"] // 2, size["y"] // 2)

    def come_round(sign, k):
        if ("z", sign, k) not in here:
            here.add(("z", sign, k))
            turned[sign, k].wait_recv()

    def go_round(k):
        for sign in (1, -1):
            if k:
                come_round(sign, k - 1)
            block = wg[0].at[me["x"], along("z", -sign * k)]
            if k == most - 1:
                block = block.at[part_of(sign)]
            copy = remote(block, block, ("g2", 0, sign, k), ("g2", 0), at("z", along("z", sign)))
            copy.start()
            turned[sign, k] = copy

    def forward(p, sign, k, o):
        a1, a2, a3 = ORDERS[p]
        if p == 0 and k == 0 and o:
            hops = min(o, size[a2] - o)
            for way in (1, -1):
                if hops == most or (o > most) == (way > 0):
                    come_round(way, hops - 1)
        elif k == 0 and o and (p, o) not in here:
            here.add((p, o))
            arrived(wg[p].at[0, 0], "g2", p, o)
        if k > 0:
            going[p, sign, k - 1, o].wait_recv()
            waited.add((p, sign, k - 1, o))
        block = wg[p].at[along(a3, -sign * k), along(a2, o)]
        copy = remote(block, block, ("g3", p, sign, k, o), ("g3", p), at(a3, along(a3, sign)))
        copy.start()
        going[p, sign, k, o] = copy

    def gather_hops(p, sign):
        a1, a2, a3 = ORDERS[p]
        steps, order = size[a3] // 2, offsets(a2)
        return [(k, o) for k in range(steps - 1) for o in order] + [
            (steps - 1, o) for o in halves(a2, sign, order)
        ]

    def gathered(p):
        for key, copy in going.items():
            if key[0] == p and key not in waited:
                copy.wait_recv()

    second(1)
    second(2)
    masks(0)
    lax.fori_loop(0, seqs, turn(0), 0)
    query_order = offsets(ORDERS[0][1])
    lists = [(p, sign, gather_hops(p, sign)) for p in (1, 2) for sign in (1, -1)]
    for turn_at in range(max(len(hops) for _, _, hops in lists)):
        for p, sign, hops in lists:
            if turn_at < len(hops):
                forward(p, sign, *hops[turn_at])
        if turn_at == 3:
            arrived(wg[0].at[0, 0, pl.ds(0, size["y"] - 1)], "g1", 0)
        if turn_at % 8 == 3:
            go_round(turn_at // 8)
        if turn_at % 8 == 5 and turn_at > 8:
            third = turn_at // 8
            for o in query_order[2 * third - 1 - (third == 1) : 2 * third + 1]:
                for sign in (1, -1):
                    forward(0, sign, 0, o)
        if turn_at == size["y"] - 1:
            swap_x.wait_recv()
        if turn_at >= size["y"]:
            done = (turn_at - size["y"]) * 2
            if done < seqs:
                lax.fori_loop(done, done + 2, turn(1), 0)

    swap_s.wait_recv()
    masks(1)
    ours = jnp.where(s < seqs // 2, starts[0], starts[1])

    def fill(r, _):
        low = (r * rows).astype(F32)
        inside = jnp.where((ours >= low) & (ours < low + rows), 1.0, 0.0)
        none = 1.0 - jnp.max(inside, axis=0)
        keep[r] = jnp.concatenate([none] * (keep.shape[1] // 8), axis=0)
        return 0

    lax.fori_loop(0, seqs, fill, 0)
    swap_c.wait_recv()
    query_last = {sign: halves(ORDERS[0][1], sign, query_order) for sign in (1, -1)}
    for o in query_order[5:-1]:
        for sign in (1, -1):
            forward(0, sign, 0, o)
    for o in query_last[1][:-1]:
        forward(0, 1, 1, o)
    gathered(1)
    gathered(2)
    for sign in (1, -1):
        forward(0, sign, 0, query_order[-1])

    def tokens_of(zz):
        at_chunk = pl.ds(pl.multiple_of(zz * 2 * chunk, 2 * chunk), 2 * chunk)
        return x2[:, :, at_chunk].reshape(2 * rows, 2 * chunk)

    def project_kv(zz, acc):
        for xh in range(2):
            pair = pl.ds(2 * xh, 2)
            wkv[zz, xh * chunk : (xh + 1) * chunk, :HEAD] = wg[1][zz, :, pair].reshape(chunk, HEAD)
            wkv[zz, xh * chunk : (xh + 1) * chunk, HEAD:] = wg[2][:, zz, pair].reshape(chunk, HEAD)
        return acc + dot(tokens_of(zz), wkv[zz])

    def project_q(zz, acc):
        for xh in range(2):
            part = jnp.stack([wg[0][2 * xh, zz], wg[0][2 * xh + 1, zz]], axis=1).reshape(chunk, HEAD)
            wq[zz, xh * chunk : (xh + 1) * chunk] = part
        return acc + dot(tokens_of(zz), wq[zz])

    acc = lax.fori_loop(0, size["z"], project_kv, jnp.zeros((2 * rows, 2 * HEAD), F32))
    proj[:, :, HEAD:] = acc.astype(BF16).reshape(2, rows, 2 * HEAD)

    shrink = 1.0 / HEAD

    def block(b, p):
        return proj[b, :, p * HEAD : (p + 1) * HEAD]

    deep = 2 * HEAD // seqs

    def send_slices(source, key):
        def send(i, _):
            k = seqs // 2 + (2 * lax.rem(i, 2) - 1) * ((i + 1) // 2)
            place = lax.rem(s + k, seqs)
            remote(scan.at[source, place], scan.at[source + 1, s], (key,), (key,), (place, d)).start()
            return 0

        lax.fori_loop(0, seqs - 1, send, 0)
        scan[source + 1, s] = scan[source, s]

    def take_slices(source, key):
        arrived(scan.at[source + 1, pl.ds(0, seqs - 1)], key)

    def sweep(source, backward):
        def step(i, run):
            r = seqs - 1 - i if backward else i
            scan[source + 2, r] = run.astype(BF16)
            return run * keep[r] + scan[source + 1, r].astype(F32)

        lax.fori_loop(0, seqs, step, jnp.zeros((deep, HEAD), F32))

    def give(slot, b, state):
        scan[slot, pl.ds(b * seqs // 2, seqs // 2)] = state.astype(BF16).reshape(seqs // 2, deep, HEAD)

    for b in range(2):
        tail = (mask[b, 2] * block(b, 1).astype(F32)).astype(BF16)
        give(0, b, dot_tn(tail, block(b, 2)))
    send_slices(0, "f1")
    forward(0, 1, 1, query_last[1][-1])
    for o in query_last[-1]:
        forward(0, -1, 1, o)
    take_slices(0, "f1")
    sweep(0, False)
    send_slices(2, "f2")
    gathered(0)
    acc = lax.fori_loop(0, size["z"], project_q, jnp.zeros((2 * rows, HEAD), F32))
    proj[:, :, :HEAD] = acc.astype(BF16).reshape(2, rows, HEAD)
    for b in range(2):
        weak[b] = (mask[b, 0] * (shrink * dot_nt(block(b, 0), block(b, 1)))).astype(BF16)
        hold[b] = dot(weak[b], block(b, 2))
    take_slices(2, "f2")
    def state(slot, b):
        return scan[slot, pl.ds(b * seqs // 2, seqs // 2)].reshape(HEAD, HEAD)

    for b in range(2):
        leading = mask[b, 1]
        q = block(b, 0)
        attended = hold[b] + leading * (shrink * dot(q, state(3, b)))
        inverse = lax.rsqrt(jnp.mean(attended * attended, axis=1, keepdims=True) + 1.0)
        result = (attended * inverse).astype(BF16)
        if b == 0:
            kept_n[...] = result
        else:
            nsend[...] = result
        upstream = cots[b].astype(F32)
        mean = jnp.mean(upstream * attended, axis=1, keepdims=True)
        grad = (inverse * upstream - attended * (inverse * inverse * inverse * mean)).astype(BF16)
        cots[b] = grad
        head = (leading * q.astype(F32)).astype(BF16)
        give(4, b, dot_tn(head, grad))
    send_slices(4, "r1")
    swap_n = remote(nsend, nrecv, ("n",), ("n",), sibling)
    swap_n.start()
    for b in range(2):
        grad = cots[b]
        mixed = (mask[b, 0] * (shrink * dot_nt(grad, block(b, 2)))).astype(BF16)
        grad_q = dot(mixed, block(b, 1)) + mask[b, 1] * (shrink * dot_nt(grad, state(3, b)))
        gbuf[b, :, 0:HEAD] = grad_q.astype(BF16)
        held[b, 0] = dot_tn(mixed, block(b, 0))
        held[b, 1] = dot_tn(weak[b], grad)

    def outer_q(zz, _):
        at_chunk = pl.ds(pl.multiple_of(zz * 2 * chunk, 2 * chunk), 2 * chunk)
        part = dot(xt[at_chunk, :], gbuf[:, :, :HEAD].reshape(2 * rows, HEAD)).astype(BF16)
        part = part.reshape(2, size["y"], 2, ROWS, HEAD)
        for xh in range(2):
            for xl in range(2):
                pg[0][2 * xh + xl, zz] = part[xh, :, xl]
        return 0

    def outer_kv(zz, _):
        at_chunk = pl.ds(pl.multiple_of(zz * 2 * chunk, 2 * chunk), 2 * chunk)
        part = dot(xt[at_chunk, :], gbuf[:, :, HEAD:].reshape(2 * rows, 2 * HEAD)).astype(BF16)
        for xh in range(2):
            pair = pl.ds(2 * xh, 2)
            some = part[xh * chunk : (xh + 1) * chunk]
            pg[1][zz, :, pair] = some[:, :HEAD].reshape(size["y"], 2, ROWS, HEAD)
            pg[2][:, zz, pair] = some[:, HEAD:].reshape(size["y"], 2, ROWS, HEAD)
        return 0

    def inner(i, _):
        at_chunk = pl.ds(pl.multiple_of(i * 2 * chunk, 2 * chunk), 2 * chunk)
        part = dot_nt(gbuf[:, :, :HEAD].reshape(2 * rows, HEAD), wq[i])
        part = part + dot_nt(gbuf[:, :, HEAD:].reshape(2 * rows, 2 * HEAD), wkv[i])
        gown[:, at_chunk] = part[:rows]
        gsend[:, at_chunk] = part[rows:].astype(BF16)
        return 0

    def sum_hops(p, sign):
        a1, a2, a3 = ORDERS[p]
        steps, order = size[a3] // 2, offsets(a2)[::-1]
        some = halves(a2, sign, order)
        hops = [(0, o) for o in some]
        if steps > 1:
            hops += [(1, o) for o in order if o not in some] + [(1, o) for o in some]
        return hops + [(k, o) for k in range(2, steps) for o in order]

    coming = {}

    def slot(p, sign, k, o):
        return ring[p].at[0 if sign > 0 else 1, k, along(ORDERS[p][1], o)]

    def pass_on(p, sign, k, o):
        a1, a2, a3 = ORDERS[p]
        mine = pg[p].at[along(a3, sign * (size[a3] // 2 - k)), along(a2, o)]
        if (p, sign, k - 1, o) in coming:
            coming[p, sign, k - 1, o].wait_recv()
            mine[...] = (mine[...].astype(F32) + slot(p, sign, k - 1, o)[...].astype(F32)).astype(BF16)
        arrival = ("g3", p, -sign, size[a3] // 2 - 1 - k, o) if p == 1 else ("r3", p, sign, k, o)
        copy = remote(mine, slot(p, sign, k, o), arrival, ("r3", p), at(a3, along(a3, sign)))
        copy.start()
        coming[p, sign, k, o] = copy

    def settle(p, o):
        a1, a2, a3 = ORDERS[p]
        mine = pg[p].at[me[a3], along(a2, o)]
        total = mine[...].astype(F32)
        for sign in (1, -1):
            key = (p, sign, size[a3] // 2 - 1, o)
            if key in coming:
                coming[key].wait_recv()
                total = total + slot(*key)[...].astype(F32)
        mine[...] = total.astype(BF16)
        if o and p:
            remote(mine, far[p].at[me[a2]], ("r2", p), ("r2", p), at(a2, along(a2, o))).start()

    summing = {}

    def sum_round(k):
        for sign in (1, -1):
            mine = pg[0].at[me["x"], along("z", sign * (most - k))]
            base_slot = 0 if sign > 0 else most
            there = far[0].at[base_slot + k]
            if k:
                summing[sign, k - 1].wait_recv()
                rows_in = part_of(sign) if k == 1 else pl.ds(0, size["y"])
                piece = mine.at[rows_in]
                came = far[0][base_slot + k - 1, rows_in].astype(F32)
                piece[...] = (piece[...].astype(F32) + came).astype(BF16)
            else:
                mine, there = mine.at[part_of(sign)], there.at[part_of(sign)]
            copy = remote(mine, there, ("r2", 0, sign, k), ("r2", 0), at("z", along("z", sign)))
            copy.start()
            summing[sign, k] = copy

    def first_sends(p, total):
        a1, a2, a3 = ORDERS[p]
        mine = pg[p].at[me[a3], me[a2]]
        mine[...] = total.astype(BF16)
        for o in offsets(a1)[:0:-1]:
            place = along(a1, o)
            remote(mine.at[place], near[p].at[me[a1]], ("r1", p), ("r1", p), at(a1, place)).start()

    def sum_end():
        total = pg[0][me["x"], me["z"]].astype(F32)
        for sign in (1, -1):
            summing[sign, most - 1].wait_recv()
            total = total + far[0][(0 if sign > 0 else most) + most - 1].astype(F32)
        first_sends(0, total)

    def settle_second(p):
        a1, a2, a3 = ORDERS[p]
        arrived(far[p].at[pl.ds(0, size[a2] - 1)], "r2", p)
        mine = pg[p].at[me[a3], me[a2]]
        total = mine[...].astype(F32)
        for k in range(1, size[a2]):
            total = total + far[p][along(a2, k)].astype(F32)
        first_sends(p, total)

    lax.fori_loop(0, size["z"], outer_q, 0)
    steps_q = {sign: sum_hops(0, sign) for sign in (1, -1)}
    free = size[ORDERS[0][1]]
    for i in range(free):
        for sign in (1, -1):
            pass_on(0, sign, *steps_q[sign][i])
    take_slices(4, "r1")
    sweep(4, True)
    send_slices(6, "r2s")
    for i in range(free, len(steps_q[1])):
        for sign in (1, -1):
            pass_on(0, sign, *steps_q[sign][i])
    take_slices(6, "r2s")
    for b in range(2):
        trailing = mask[b, 2] * shrink
        grad_k = held[b, 0] + trailing * dot_nt(block(b, 2), state(7, b))
        grad_v = held[b, 1] + trailing * dot(block(b, 1), state(7, b))
        gbuf[b, :, HEAD : 2 * HEAD] = grad_k.astype(BF16)
        gbuf[b, :, 2 * HEAD :] = grad_v.astype(BF16)
    lax.fori_loop(0, size["z"], outer_kv, 0)

    lists = [(p, sign, sum_hops(p, sign)) for p in (1, 2) for sign in (1, -1)]
    turns = max(len(hops) for _, _, hops in lists)
    done = 0
    for turn_at in range(turns):
        for p, sign, hops in lists:
            if turn_at < len(hops):
                pass_on(p, sign, *hops[turn_at])
        upto = min(size["z"] // 2, size["z"] * (turn_at + 1) // (turns + 1))
        if upto > done:
            lax.fori_loop(done, upto, inner, 0)
            done = upto
        if turn_at == 1:
            for o in offsets(ORDERS[0][1])[::-1]:
                settle(0, o)
        if turn_at % 8 == 1:
            sum_round(turn_at // 8)
    for o in offsets(ORDERS[1][1])[::-1]:
        settle(1, o)
        settle(2, o)
    sum_end()
    swap_n.wait_recv()
    mine, other = kept_n[...].astype(F32), nrecv[...].astype(F32)
    normed[:, :HEAD] = jnp.where(first, mine, other).astype(BF16)
    normed[:, HEAD:] = jnp.where(first, other, mine).astype(BF16)
    stores = [pltpu.make_async_copy(normed, normed_hbm, load_sem.at[4])]
    stores[0].start()
    lax.fori_loop(done, size["z"], inner, 0)
    swap_g = remote(gsend, grecv, ("gi",), ("gi",), sibling)
    swap_g.start()
    settle_second(1)
    settle_second(2)
    swap_g.wait_recv()

    def close(i, _):
        at_chunk = pl.ds(pl.multiple_of(i * chunk, chunk), chunk)
        grecv[:, at_chunk] = (gown[:, at_chunk] + grecv[:, at_chunk].astype(F32)).astype(BF16)
        return 0

    lax.fori_loop(0, seqs, close, 0)
    stores.append(pltpu.make_async_copy(grecv, gin_hbm, load_sem.at[5]))
    stores[1].start()
    factor = 1.0 / math.sqrt(size["y"] * 4 * seqs * rows)
    kept = []
    for p, (a1, a2, a3) in enumerate(ORDERS):
        arrived(near[p].at[pl.ds(0, size[a1] - 1)], "r1", p)
        total = pg[p][me[a3], me[a2], me[a1]].astype(F32)
        for k in range(1, size[a1]):
            total = total + near[p][along(a1, k)].astype(F32)
        total = factor * total
        kept.append(jnp.where(first, total[:8], total[8:]))
        dsend[:, p * HEAD : (p + 1) * HEAD] = jnp.where(first, total[8:], total[:8])
    swap_d = remote(dsend, drecv, ("d",), ("d",), sibling)
    swap_d.start()
    for p, (a1, a2, a3) in enumerate(ORDERS):
        departed(wg[p].at[0, 0, pl.ds(0, size[a1] - 1)], "g1", p)
        departed(wg[p].at[0, pl.ds(0, size[a2] - 1)], "g2", p)
        departed(wg[p].at[pl.ds(0, size[a3] - 1)], "g3", p)
        departed(pg[p].at[pl.ds(0, size[a3] - 1)], "r3", p)
        departed(far[p].at[pl.ds(0, size[a2] - 1)], "r2", p)
        departed(near[p].at[pl.ds(0, size[a1] - 1)], "r1", p)
    for i, key in enumerate(("f1", "f2", "r1", "r2s")):
        departed(scan.at[2 * i, pl.ds(0, seqs - 1)], key)
    for copy in (swap_w, swap_x, swap_c, swap_s, swap_n, swap_g):
        copy.wait_send()
    swap_d.wait()
    columns = []
    for p in range(3):
        other = drecv[:, p * HEAD : (p + 1) * HEAD]
        columns += [jnp.where(first, kept[p], other), jnp.where(first, other, kept[p])]
    gw[...] = jnp.concatenate(columns, axis=1).astype(BF16)
    stores.append(pltpu.make_async_copy(gw, gw_hbm, load_sem.at[6]))
    stores[2].start()
    for store in stores:
        store.wait()
    assert len(names) <= recv_sem.shape[0] and len(sends) <= send_sem.shape[0]


def deliver(normed, gin, gw, normed_out, gin_out, gw_out, sem):
    parts = 4
    span = gin.shape[0] // parts
    copies = [pltpu.make_async_copy(normed, normed_out, sem.at[0]), pltpu.make_async_copy(gw, gw_out, sem.at[1])]
    for i in range(parts):
        rows = pl.ds(i * span, span)
        copies.append(pltpu.make_async_copy(gin.at[rows], gin_out.at[rows], sem.at[2 + i]))
    for copy in copies:
        copy.start()
    for copy in copies:
        copy.wait()


def solution(mesh):
    seqs, dps = mesh.shape["seq"], mesh.shape["dp"]
    size = {"x": 4, "y": dps // 4, "z": seqs // 2}

    def shards(inputs, weights, lengths, cotangent):
        tokens = inputs[0]
        rows, width = tokens.shape
        chunk = width // seqs
        wide = 3 * HEAD
        shapes = []
        for order in ORDERS:
            shapes.append(tuple(size[a] for a in order[::-1]) + (ROWS, HEAD))
        scratch = [
            pltpu.VMEM((2, rows, width), BF16),
            pltpu.VMEM((8, 2 * wide), BF16),
            pltpu.VMEM((rows, 2 * HEAD), BF16),
            pltpu.SMEM((1, NDOC), jnp.int32),
            pltpu.VMEM((width, 2 * rows), BF16),
            pltpu.VMEM((seqs // 2, 2 * chunk, HEAD), BF16),
            pltpu.VMEM((seqs // 2, 2 * chunk, 2 * HEAD), BF16),
            pltpu.VMEM((8, wide), F32),
            pltpu.VMEM((8, wide), F32),
            pltpu.VMEM((2, NDOC, 8, HEAD), F32),
            pltpu.VMEM((rows, HEAD), BF16),
            pltpu.VMEM((2, rows, HEAD), BF16),
            pltpu.VMEM((2, rows, wide), BF16),
            pltpu.VMEM((8, seqs, 2 * HEAD // seqs, HEAD), BF16),
            pltpu.VMEM((seqs, 2 * HEAD // seqs, HEAD), F32),
            pltpu.VMEM((2, rows, wide), BF16),
            pltpu.VMEM((2, 3, rows, rows), F32),
            pltpu.VMEM((2, rows, rows), BF16),
            pltpu.VMEM((2, rows, HEAD), F32),
            pltpu.VMEM((2, 2, rows, HEAD), F32),
            pltpu.VMEM((rows, HEAD), BF16),
            pltpu.VMEM((rows, HEAD), BF16),
            pltpu.VMEM((rows, HEAD), BF16),
            pltpu.VMEM((rows, width), F32),
            pltpu.VMEM((rows, width), BF16),
            pltpu.VMEM((rows, width), BF16),
            pltpu.VMEM((8, wide), F32),
            pltpu.VMEM((8, wide), F32),
            pltpu.VMEM((rows, 2 * HEAD), BF16),
            pltpu.VMEM((8, 2 * wide), BF16),
            pltpu.SemaphoreType.DMA((7,)),
            pltpu.SemaphoreType.DMA((29,)),
            pltpu.SemaphoreType.DMA((265,)),
        ]
        scratch += [pltpu.VMEM(shape, BF16) for shape in shapes]
        scratch += [pltpu.VMEM(shape, BF16) for shape in shapes]
        scratch += [pltpu.VMEM((2, shape[0] // 2) + shape[1:], BF16) for shape in shapes]
        scratch += [pltpu.VMEM(shape[1:], BF16) for shape in shapes]
        scratch += [pltpu.VMEM(shape[2:], BF16) for shape in shapes]
        hbm = pl.BlockSpec(memory_space=pltpu.HBM)
        results = (
            jax.ShapeDtypeStruct((rows, 2 * HEAD), BF16),
            jax.ShapeDtypeStruct((rows, width), BF16),
            jax.ShapeDtypeStruct((8, 2 * wide), BF16),
        )
        found = pl.pallas_call(
            functools.partial(kernel, size),
            out_shape=results,
            in_specs=[hbm] * 4,
            out_specs=(hbm, hbm, hbm),
            scratch_shapes=scratch,
            compiler_params=pltpu.CompilerParams(
                collective_id=0, has_side_effects=True, vmem_limit_bytes=56 * 1024 * 1024
            ),
            cost_estimate=pl.CostEstimate(flops=3 * 10**9, bytes_accessed=4 * 10**6, transcendentals=0),
        )(tokens, weights, lengths, cotangent[0])
        normed, gin, gw = pl.pallas_call(
            deliver,
            out_shape=results,
            in_specs=[pl.BlockSpec(memory_space=pltpu.VMEM)] * 3,
            out_specs=(hbm, hbm, hbm),
            scratch_shapes=[pltpu.SemaphoreType.DMA((6,))],
        )(*found)
        return normed[None], gin[None], gw

    placed = (P("dp", "seq", None), P(("seq", "dp"), None), P("dp", None), P("dp", "seq", None))
    return jax.shard_map(
        shards,
        mesh=mesh,
        in_specs=placed,
        out_specs=(P("dp", "seq", None), P("dp", "seq", None), P(("seq", "dp"), None)),
        check_vma=False,
    )
```
